32 devices in a mesh: energy: 8 (over z, core), seg: 4 (over y, x).
Axes of the slice: x: 2, y: 2, z: 4, core: 2. Of those that a mesh axis runs over, the one named last changes fastest.
Arguments:
- energies: float32 [8], P('energy'), may hold values from -2 to 2
- h_blocks: float32 [4, 4, 64, 128], P('seg'), as said below
- couplings: float32 [4, 4, 64, 128], P('seg')
- shift_real: float32 [8, 4, 256], P('energy', 'seg'), may hold values from -0.625 to 0.625
- shift_rate: float32 [8, 4, 256], P('energy', 'seg'), may hold values from 0.005 to 0.05
- screened: float32 [8, 4, 4, 64, 128], P(None, 'seg'), may hold values from -3 to 3
- sources: int32 [8, 8], P('energy'), may hold values from 0 to 7, as said below
- counts: int32 [4], P('seg'), may hold values from 1 to 4, 8 in all
Outputs:
- sigma_new: float32 [8, 4, 4, 64, 128], P('energy', 'seg')
The draws below stay inside these ranges and needn't reach their ends.
Inputs may be any that keep to these rules, and one draw needn't show every extreme that they name: `h_blocks`: each diagonal block is Hermitian: its real part symmetric, its imaginary part antisymmetric. The counts sum to 8; some segment holds exactly 4 blocks. For every group of 1 consecutive energies starting at a multiple of 1, its 8 sources lie at most 1 in any one such group, and exactly 1 in some group.
All inputs are finite; a program needn't handle non-finite values.
Results may differ from the reference program's by a relative error of at most 0.0029.
Values may be sent and summed in bfloat16 or wider, within the bound.
No kernel may reach another device: no remote copies, remote signals or barrier semaphores. Data moves between devices by JAX's collectives and lax.ppermute only.
A program may use at most 64 MiB of HBM per device.

```python
import math
import jax
import jax.numpy as jnp
import numpy as np
from jax import lax

BS = 64
MAXB = 4
NSHIFT = 8
E_DEV = 1
SEGS = 4
ENERGIES = 8
PULL = 1


def hermitian_from(real_draw, imag_draw, factor):
    real_part = (real_draw + jnp.swapaxes(real_draw, -1, -2)) * (0.5 * factor)
    imag_part = (imag_draw - jnp.swapaxes(imag_draw, -1, -2)) * (0.5 * factor)
    return jnp.concatenate([real_part, imag_part], -1)


def draw_h_blocks(key, part):
    keys = jax.random.split(jax.random.fold_in(key, 11), 4)
    common_shape = (BS, BS)
    spread_shape = (SEGS, MAXB, BS, BS)
    common_real = jax.random.normal(keys[0], common_shape, jnp.float32)
    common_imag = jax.random.normal(keys[1], common_shape, jnp.float32)
    spread_real = jax.random.normal(keys[2], spread_shape, jnp.float32)
    spread_imag = jax.random.normal(keys[3], spread_shape, jnp.float32)
    common = hermitian_from(common_real, common_imag, 0.75 / math.sqrt(BS))
    spread = hermitian_from(spread_real, spread_imag, 0.1 / math.sqrt(BS))
    return common[None, None] + spread


def draw_couplings(key, part):
    common_key, spread_key = jax.random.split(jax.random.fold_in(key, 13))
    common = jax.random.normal(common_key, (BS, 2 * BS), jnp.float32)
    spread = jax.random.normal(spread_key, (SEGS, MAXB, BS, 2 * BS), jnp.float32)
    return common[None, None] * (0.32 / math.sqrt(BS)) + spread * (0.035 / math.sqrt(BS))


def shuffled_slots(row_key):
    groups = ENERGIES // E_DEV
    return jax.random.permutation(row_key, groups * PULL)


def draw_sources(key, part):
    order_key, pick_key = jax.random.split(jax.random.fold_in(key, 17))
    groups = ENERGIES // E_DEV
    requests = E_DEV * NSHIFT
    row_keys = jax.random.split(order_key, groups)
    slots = jax.vmap(shuffled_slots)(row_keys)[:, :requests]
    owner_of = slots % groups
    within = jax.random.randint(pick_key, (groups, requests), 0, E_DEV)
    return (owner_of * E_DEV + within).astype(jnp.int32).reshape(ENERGIES, NSHIFT)


def level_of(key, extent, shards, low, largest):
    def one(dim, blocks):
        steps = jax.random.uniform(jax.random.fold_in(jax.random.fold_in(key, 6), dim), (blocks,), jnp.float32, low / len(shards), largest / len(shards))
        return jnp.repeat(jnp.exp(steps), extent[dim] // blocks).reshape((-1,) + (1,) * (len(extent) - dim - 1))

    factor_of = one(*shards[0])
    for cut in shards[1:]:
        factor_of = factor_of * one(*cut)
    return factor_of


def split_up(number_of, total, reach, lean):
    loads = [(1 << 20) // math.isqrt(grade ** lean) + 1 for grade in range(2, number_of + 1)]
    surplus, given = total - reach - (number_of - 1), [1] * (number_of - 1)
    while surplus > 0:
        candidates = [i for i in range(number_of - 1) if given[i] < reach]
        pool, budget = sum([loads[i] for i in candidates]), surplus
        for i in candidates:
            more = min(reach - given[i], max(1, budget * loads[i] // pool), surplus)
            given[i] = given[i] + more
            surplus = surplus - more
    return np.array([reach] + given)


def ragged(key, amount, total, limit, lean):
    if amount == 2:
        one = jax.random.randint(key, (), max(1, total - limit), min(limit, total - 1) + 1)
        return jnp.stack([one, total - one])
    tallies = jnp.asarray(split_up(amount, total, limit, lean), jnp.int32)
    pairs = (amount - 1) // 2
    giver, receiver = tallies[1:1 + 2 * pairs:2], tallies[2:2 + 2 * pairs:2]
    margin = jnp.minimum(giver - 1, limit - receiver)
    moved = jax.random.randint(jax.random.fold_in(key, 1), (pairs,), 0, 1 << 20) % (margin + 1)
    tallies = tallies.at[1:1 + 2 * pairs:2].set(giver - moved).at[2:2 + 2 * pairs:2].set(receiver + moved)
    return tallies[jax.random.permutation(jax.random.fold_in(key, 2), amount)]


def gaussian(rng, extent, scale, limit, shards=(), kind=jnp.bfloat16):
    entries = jax.random.normal(rng, extent, jnp.float32) * scale
    if len(shards) > 0:
        entries = level_of(rng, extent, shards, -0.22, 0.18) * entries
    return jnp.clip(entries, min=-limit, max=limit).astype(kind)


def setup_inputs(seed: int = 0) -> dict:
    key_list = jax.random.split(jax.random.key(seed), 9)
    return {
        "energies": jnp.clip(jax.random.uniform(key_list[0], (ENERGIES,), jnp.float32, -2.0, 2.0) * level_of(key_list[0], (ENERGIES,), ((0, 8),), -0.4, 0.0), -2.0, 2.0),
        "h_blocks": draw_h_blocks(jax.random.fold_in(key_list[8], 71), 0),
        "couplings": draw_couplings(jax.random.fold_in(key_list[8], 71), 0),
        "shift_real": gaussian(key_list[3], (ENERGIES, SEGS, MAXB * BS), 0.1, 0.625, ((0, 8), (1, 4)), jnp.float32),
        "shift_rate": jnp.clip(jnp.exp(math.log(0.05) - 2.3025851 * jax.random.uniform(key_list[4], (ENERGIES, SEGS, MAXB * BS), jnp.float32) ** level_of(key_list[4], (ENERGIES, SEGS, MAXB * BS), ((0, 8), (1, 4)), -0.2, 0.2)), 0.005, 0.05),
        "screened": gaussian(key_list[5], (NSHIFT, SEGS, MAXB, BS, 2 * BS), 0.5, 3.0, ((1, 4),), jnp.float32),
        "sources": draw_sources(jax.random.fold_in(key_list[8], 71), 0),
        "counts": ragged(key_list[7], SEGS, 2 * SEGS, MAXB, 2).astype(jnp.int32),
    }


broadening = 0.02

def expand(matrix):
    order = matrix.shape[-2]
    real_part = matrix[..., :order]
    imag_part = matrix[..., order:]
    return jnp.concatenate([jnp.concatenate([real_part, imag_part], -1), jnp.concatenate([-imag_part, real_part], -1)], -2)

def complex_product(matrix, other):
    return jnp.matmul(matrix, expand(other), precision=lax.Precision.HIGHEST)

def adjoint(matrix):
    order = matrix.shape[-2]
    return jnp.concatenate([jnp.swapaxes(matrix[..., :order], -1, -2), -jnp.swapaxes(matrix[..., order:], -1, -2)], -1)

def complex_inverse(matrix):
    order = matrix.shape[-2]
    real_part = matrix[..., :order]
    imag_part = matrix[..., order:]
    real_form = jnp.concatenate([jnp.concatenate([real_part, -imag_part], -1), jnp.concatenate([imag_part, real_part], -1)], -2)
    flipped = jnp.swapaxes(real_form, -1, -2)
    normal = jnp.matmul(flipped, real_form, precision=lax.Precision.HIGHEST)
    factor = jnp.linalg.cholesky(normal)
    middle = jax.scipy.linalg.solve_triangular(factor, flipped[..., :order], lower=True)
    solved = jax.scipy.linalg.solve_triangular(factor, middle, lower=True, trans=1)
    return jnp.concatenate([solved[..., :order, :], solved[..., order:, :]], -1)

def unit_block(order):
    return jnp.concatenate([jnp.eye(order, dtype=jnp.float32), jnp.zeros((order, order), jnp.float32)], -1)

def entry_product(green, weight):
    order = green.shape[-2]
    green_re = green[..., :order]
    green_im = green[..., order:]
    weight_re = weight[..., :order]
    weight_im = weight[..., order:]
    return jnp.concatenate([green_re * weight_re - green_im * weight_im, green_re * weight_im + green_im * weight_re], -1)

def build_blocks(energies, hams, shift_real, shift_rate):
    slots, order = (hams.shape[0], hams.shape[1])
    batch = energies.shape[0]
    identity = jnp.eye(order, dtype=jnp.float32)
    shifts = shift_real.reshape(batch, slots, order)
    rates = shift_rate.reshape(batch, slots, order)
    real_part = energies[:, None, None, None] * identity - hams[None, :, :, :order] - shifts[..., :, None] * identity
    imag_part = broadening * identity - hams[None, :, :, order:] + rates[..., :, None] * identity
    return jnp.concatenate([real_part, imag_part], -1)

def segment_summary(diag_a, links, used_blocks):
    slots = diag_a.shape[1]
    last_block = complex_inverse(diag_a[:, 0])
    head_block, upper_block, lower_block = (last_block, last_block, last_block)
    for k in range(1, slots):
        link_block = links[k]
        back_link = adjoint(link_block)
        fresh_block = complex_inverse(diag_a[:, k] - complex_product(complex_product(back_link, last_block), link_block))
        left_part = complex_product(upper_block, link_block)
        right_part = complex_product(back_link, lower_block)
        new_upper = complex_product(left_part, fresh_block)
        new_lower = complex_product(fresh_block, right_part)
        new_head = head_block + complex_product(new_upper, right_part)
        live = k < used_blocks
        head_block = jnp.where(live, new_head, head_block)
        upper_block = jnp.where(live, new_upper, upper_block)
        lower_block = jnp.where(live, new_lower, lower_block)
        last_block = jnp.where(live, fresh_block, last_block)
    return (head_block, upper_block, lower_block, last_block)

def pick_blocks(flag, first_item, second_item):
    return jnp.where(flag[..., None, None] > 0.5, first_item, second_item)

def join_segments(left_group, right_group):
    a, b, c, d, entry_a, flag_a = left_group
    p, q, r, s, link_v, flag_b = right_group
    back_v = adjoint(link_v)
    order = a.shape[-2]
    cross_term = complex_product(complex_product(back_v, d), link_v)
    resolvent = complex_inverse(unit_block(order) - complex_product(p, cross_term))
    res_first = complex_product(resolvent, p)
    res_upper = complex_product(resolvent, q)
    d_link = complex_product(d, link_v)
    back_c = complex_product(back_v, c)
    b_link = complex_product(b, link_v)
    head_block = a + complex_product(complex_product(b_link, res_first), back_c)
    upper_block = complex_product(b_link, res_upper)
    k_lower = c + complex_product(complex_product(d_link, res_first), back_c)
    lower_block = complex_product(r, complex_product(back_v, k_lower))
    last_block = s + complex_product(complex_product(r, cross_term), res_upper)
    joined = (head_block, upper_block, lower_block, last_block, entry_a)
    result = tuple((pick_blocks(flag_a, rb, pick_blocks(flag_b, lb, jb)) for lb, rb, jb in zip(left_group[:5], right_group[:5], joined)))
    return result + (flag_a * flag_b,)

def segment_greens(diag_a, links, used_blocks, previous, sig_right):
    slots = diag_a.shape[1]
    forward_blocks = []
    for k in range(slots):
        link_block = links[k]
        inner_block = diag_a[:, k] - complex_product(complex_product(adjoint(link_block), previous), link_block) - jnp.where(k == used_blocks - 1, sig_right, 0.0)
        fresh_block = complex_inverse(inner_block)
        forward_blocks.append(fresh_block)
        previous = fresh_block
    greens = list(forward_blocks)
    for k in range(slots - 2, -1, -1):
        link_block = links[k + 1]
        spread = complex_product(forward_blocks[k], link_block)
        updated = forward_blocks[k] + complex_product(complex_product(spread, greens[k + 1]), complex_product(adjoint(link_block), forward_blocks[k]))
        greens[k] = jnp.where(k <= used_blocks - 2, updated, forward_blocks[k])
    greens = [jnp.where(k < used_blocks, greens[k], 0.0) for k in range(slots)]
    return jnp.stack(greens, 1)

def reference(energies, h_blocks, couplings, shift_real, shift_rate, screened, sources, counts):
    diag_a = jax.vmap(build_blocks, in_axes=(None, 0, 1, 1))(energies, h_blocks, shift_real, shift_rate)
    summaries = jax.vmap(segment_summary)(diag_a, couplings, counts)
    batch = energies.shape[0]
    entry_links = jnp.broadcast_to(couplings[:, 0][:, None], (SEGS, batch) + couplings.shape[2:])
    items = summaries + (entry_links, jnp.zeros((SEGS, batch), jnp.float32))
    zero_block = jnp.zeros((batch,) + couplings.shape[2:], jnp.float32)
    identity_item = (zero_block, zero_block, zero_block, zero_block, zero_block, jnp.ones((batch,), jnp.float32))

    def forward(running, element):
        return (join_segments(running, element), running)

    def backward(running, element):
        return (join_segments(element, running), running)
    _, before = lax.scan(forward, identity_item, items)
    _, after = lax.scan(backward, identity_item, items, reverse=True)
    right_link = after[4]
    sig_right = complex_product(complex_product(right_link, after[0]), adjoint(right_link))
    greens = jax.vmap(segment_greens)(diag_a, couplings, counts, before[3], sig_right)
    packed = jnp.swapaxes(greens, 0, 1).astype(jnp.bfloat16)
    accumulated = jnp.zeros(packed.shape, jnp.float32)
    for j in range(NSHIFT):
        picked = packed[sources[:, j]].astype(jnp.float32)
        accumulated = accumulated + entry_product(picked, screened[j][None])
    return accumulated
```

```python
import jax
import jax.numpy as jnp
from jax import lax
from jax.experimental import pallas as pl
from jax.experimental.pallas import tpu as pltpu
from jax.sharding import PartitionSpec as P

broadening = 0.02
cores = 2
f32 = jnp.float32
bf16 = jnp.bfloat16
VMEM = pl.BlockSpec(memory_space=pltpu.VMEM)
SMEM = pl.BlockSpec(memory_space=pltpu.SMEM)


def column(slab, k, lane):
    return jnp.take_along_axis(slab, jnp.where(lane < 64, k, 64 + k), axis=1)


def row(slab, k):
    return jnp.broadcast_to(slab[k : k + 1, :], (8, 128))


def added(parts):
    while len(parts) > 1:
        parts = [a + b for a, b in zip(parts[::2], parts[1::2])]
    return parts[0]


def invert_small(xr, xi, sub):
    for k in range(8):
        pr, pi = row(xr[k], k), row(xi[k], k)
        q = 1.0 / (pr * pr + pi * pi)
        ipr, ipi = pr * q, -(pi * q)
        at = sub == k
        cr, ci = xr[k], xi[k]
        for j in [(k + 1 + d) % 8 for d in range(7)]:
            ar, ai = row(xr[j], k), row(xi[j], k)
            tr = ar * ipr - ai * ipi
            ti = ar * ipi + ai * ipr
            xr[j] = jnp.where(at, tr, xr[j] - (cr * tr - ci * ti))
            xi[j] = jnp.where(at, ti, xi[j] - (cr * ti + ci * tr))
        xr[k] = jnp.where(at, ipr, ci * ipi - cr * ipr)
        xi[k] = jnp.where(at, ipi, -(cr * ipi + ci * ipr))
    return xr, xi


def pair_inverse(mr, mi):
    lane = lax.broadcasted_iota(jnp.int32, (8, 128), 1)
    sub = lax.broadcasted_iota(jnp.int32, (8, 128), 0)
    col = lane & 63
    mr, mi = list(mr), list(mi)
    for t in range(8):
        xr = [column(mr[t], 8 * t + j, lane) for j in range(8)]
        xi = [column(mi[t], 8 * t + j, lane) for j in range(8)]
        xr, xi = invert_small(xr, xi, sub)
        inside = (col >= 8 * t) & (col < 8 * t + 8)
        rr = jnp.where(inside, jnp.where(col == sub + 8 * t, 1.0, 0.0), mr[t])
        ri = jnp.where(inside, 0.0, mi[t])
        sr, si = [], []
        for j in range(8):
            br, bi = row(rr, j), row(ri, j)
            sr.append(xr[j] * br - xi[j] * bi)
            si.append(xr[j] * bi + xi[j] * br)
        pr, pi = added(sr), added(si)
        rows = [(row(pr, j), row(pi, j)) for j in range(8)]
        for s in [(t + d) % 8 for d in range(1, 8)]:
            ar, ai = [], []
            for j in range(8):
                cr, ci = column(mr[s], 8 * t + j, lane), column(mi[s], 8 * t + j, lane)
                ar.append(cr * rows[j][0] - ci * rows[j][1])
                ai.append(cr * rows[j][1] + ci * rows[j][0])
            mr[s] = jnp.where(inside, 0.0, mr[s]) - added(ar)
            mi[s] = jnp.where(inside, 0.0, mi[s]) - added(ai)
        mr[t], mi[t] = pr, pi
    return mr, mi


def slabs(x):
    return [x[8 * s : 8 * s + 8] for s in range(8)]


def invert_pair(zr, zi):
    mr, mi = pair_inverse(slabs(zr), slabs(zi))
    return jnp.concatenate(mr, 0), jnp.concatenate(mi, 0)


def low_lanes(x):
    return lax.broadcasted_iota(jnp.int32, x.shape, 1) < 64


def split(x):
    high = x.astype(bf16)
    return high, (x - high.astype(f32)).astype(bf16)


def diagonal(x):
    keep = low_lanes(x)
    zero = jnp.zeros_like(x)
    return jnp.concatenate([jnp.where(keep, x, zero), jnp.where(keep, zero, x)], 0)


def dot(a, b):
    return jnp.dot(a, b, preferred_element_type=f32)


def left_factor(qr, qi):
    rh, rl = split(qr)
    ih, il = split(qi)

    def whole(r, i):
        return jnp.concatenate(
            [jnp.concatenate([r, -i], 1), jnp.concatenate([i, r], 1)], 0
        )

    return jnp.concatenate([whole(rh, ih), whole(rl, il)], 0)


def right_factor(yr, yi):
    def whole(r, i):
        dr, di = diagonal(r), diagonal(i)
        return jnp.concatenate(
            [jnp.concatenate([dr, di], 1), jnp.concatenate([-di, dr], 1)], 0
        )

    rh, rl = split(yr)
    ih, il = split(yi)
    return whole(rh, ih), whole(rl, il)


def times_right(xr, xi, high, low):
    xh, xl = split(jnp.concatenate([xr, xi], 1))
    both = dot(jnp.concatenate([xh, xl], 0), high)
    out = both[:64] + (both[64:] + dot(xh, low))
    return out[:, :128], out[:, 128:]


def times_left(left, xr, xi):
    rh, rl = split(xr)
    ih, il = split(xi)
    right = jnp.concatenate(
        [
            jnp.concatenate([diagonal(rh), diagonal(rl)], 1),
            jnp.concatenate([diagonal(ih), diagonal(il)], 1),
        ],
        0,
    )
    out = dot(left, right)
    out = out[:128, :128] + (out[:128, 128:] + out[128:, :128])
    return out[:64], out[64:]


def swapped(x):
    return pltpu.roll(x, 64, 1)


def pack_kernel(core_ref, counts_ref, hams_ref, links_ref, shifts_ref, rates_ref, out_ref):
    first = 2 * core_ref[0]
    out_ref[0:64] = links_ref[first]
    out_ref[64:128] = links_ref[first + 1]
    one, two = hams_ref[first], hams_ref[first + 1]
    lower = lax.broadcasted_iota(jnp.int32, (64, 128), 0) >= (
        lax.broadcasted_iota(jnp.int32, (64, 128), 1) & 63
    )
    keep = low_lanes(one)
    left = jnp.where(lower, one, swapped(one))
    right = jnp.where(lower, swapped(two), two)
    out_ref[128:192] = jnp.where(keep, left, right)
    out_ref[192:194] = shifts_ref[...]
    out_ref[194:196] = rates_ref[...]
    out_ref[196:200] = jnp.full((4, 128), counts_ref[0].astype(f32))


def pack(core, counts, hams, links, shifts, rates):
    return pl.pallas_call(
        pack_kernel,
        out_shape=jax.ShapeDtypeStruct((200, 128), f32),
        in_specs=[SMEM, SMEM, VMEM, VMEM, VMEM, VMEM],
        out_specs=VMEM,
        name="pack",
    )(core, counts, hams, links, shifts, rates)


def wire_kernel(segs, place_ref, energy_ref, *refs):
    own = refs[:segs]
    other = refs[segs : 2 * segs]
    out_ref = refs[2 * segs]
    (u_ref, h_ref, m_ref, at_ref, ar_ref, ai_ref, yright_ref, yleft_ref, g_ref, s_ref, k_ref, t_ref) = (
        refs[2 * segs + 1 :]
    )
    blocks = 2 * segs
    half = segs
    place, core = place_ref[0], place_ref[1]
    energy = energy_ref[0]

    for k in range(segs):
        seg = jnp.bitwise_xor(place, k)
        for c, ref in ((core, own[k]), (1 - core, other[k])):
            u_ref[4 * seg + 2 * c] = ref[0:64]
            u_ref[4 * seg + 2 * c + 1] = ref[64:128]
            h_ref[2 * seg + c] = ref[128:192]
        m_ref[seg] = own[k][192:200]

    start = jnp.int32(0)
    first, used = jnp.int32(0), jnp.int32(0)
    for seg in range(segs):
        count = jnp.max(m_ref[seg, 4:5, :]).astype(jnp.int32)
        for k in range(4):
            at_ref[start + k] = 4 * seg + k
        first = jnp.where(seg == place, start, first)
        used = jnp.where(seg == place, count, used)
        start = start + count

    keep = low_lanes(jnp.zeros((64, 128), f32))
    rows = lax.broadcasted_iota(jnp.int32, (64, 128), 0)
    cols = lax.broadcasted_iota(jnp.int32, (64, 128), 1) & 63

    def prepare_block(i, carry):
        one, two = at_ref[i], at_ref[blocks - 1 - i]
        odd_one, odd_two = one & 1, two & 1
        raw_one, raw_two = h_ref[one >> 1], h_ref[two >> 1]
        one_low = pltpu.roll(raw_one, 64 * odd_one, 1)
        two_low = pltpu.roll(raw_two, 64 * odd_two, 1)
        two_high = pltpu.roll(raw_two, 64 * (1 - odd_two), 1)
        packed = jnp.where(keep, one_low, two_high)
        flipped = jnp.concatenate([one_low, two_low], 0).T[:64]
        real = jnp.where(rows >= cols, packed, flipped)
        imag = jnp.where(rows < cols, packed, jnp.where(rows > cols, -flipped, 0.0))
        extra = []
        for base in (0, 2):
            line_one = m_ref[one >> 2, pl.ds(base + ((one >> 1) & 1), 1), :]
            line_two = m_ref[two >> 2, pl.ds(base + ((two >> 1) & 1), 1), :]
            line_one = pltpu.roll(jnp.broadcast_to(line_one, (8, 128)), 64 * odd_one, 1)
            line_two = pltpu.roll(jnp.broadcast_to(line_two, (8, 128)), 64 * (1 - odd_two), 1)
            line = jnp.where(keep[:8], line_one, line_two)
            extra.append(jnp.broadcast_to(line[:1], (64, 128)))
        on = rows == cols
        ar_ref[i] = jnp.where(on, energy - extra[0], 0.0) - real
        ai_ref[i] = jnp.where(on, broadening + extra[1], 0.0) - imag
        return carry

    def prepare_link(i, carry):
        one, two = u_ref[at_ref[i]], u_ref[at_ref[blocks - i]]
        flat_re = jnp.where(keep, one, swapped(two))
        flat_im = jnp.where(keep, swapped(one), two)
        turned = jnp.concatenate([one, two], 0).T
        turned_re, turned_im = turned[:64], -turned[64:]
        high, low = right_factor(
            jnp.where(keep, flat_re, turned_re), jnp.where(keep, flat_im, turned_im)
        )
        yright_ref[i - 1, 0] = high
        yright_ref[i - 1, 1] = low
        yleft_ref[i - 1] = left_factor(
            jnp.where(keep, turned_re, flat_re), jnp.where(keep, turned_im, flat_im)
        )
        return carry

    lax.fori_loop(0, half, prepare_block, 0)
    lax.fori_loop(1, half + 1, prepare_link, 0)

    s_ref[...] = jnp.zeros_like(s_ref)

    def inward(i, carry):
        fr = ar_ref[i] - s_ref[0]
        fi = ai_ref[i] - s_ref[1]
        gr, gi = invert_pair(fr, fi)
        g_ref[i, 0] = gr
        g_ref[i, 1] = gi

        @pl.when(i < half)
        def _():
            tr, ti = times_right(gr, gi, yright_ref[i, 0], yright_ref[i, 1])
            t_ref[i] = left_factor(tr, ti)
            sr, si = times_left(yleft_ref[i], tr, ti)
            kr, ki = times_left(yleft_ref[i], gr, gi)
            high, low = right_factor(kr, ki)
            k_ref[i, 0] = high
            k_ref[i, 1] = low
            s_ref[0] = sr
            s_ref[1] = si

        @pl.when(i == half - 1)
        def _():
            s_ref[0] = swapped(s_ref[0])
            s_ref[1] = swapped(s_ref[1])
            ar_ref[half] = fr
            ai_ref[half] = fi

        return carry

    lax.fori_loop(0, half + 1, inward, 0)

    g_ref[half - 1] = g_ref[half]

    def outward(step, carry):
        i = half - 2 - step
        zr, zi = times_right(g_ref[i + 1, 0], g_ref[i + 1, 1], k_ref[i, 0], k_ref[i, 1])
        wr, wi = times_left(t_ref[i], zr, zi)
        g_ref[i, 0] = g_ref[i, 0] + wr
        g_ref[i, 1] = g_ref[i, 1] + wi
        return carry

    lax.fori_loop(0, half - 1, outward, 0)

    for k in range(4):
        block = jnp.minimum(first + k, blocks - 1)
        right = (block >= half).astype(jnp.int32)
        i = jnp.where(block >= half, blocks - 1 - block, block)
        re = pltpu.roll(g_ref[i, 0], 64 * right, 1)
        im = pltpu.roll(g_ref[i, 1], 64 * (1 - right), 1)
        live = (k < used).astype(f32)
        out_ref[k] = (jnp.where(keep, re, im) * live).astype(bf16)


def wire(place, energy, own, other):
    segs = len(own)
    half = segs

    def kernel(*refs):
        wire_kernel(segs, *refs)

    return pl.pallas_call(
        kernel,
        out_shape=jax.ShapeDtypeStruct((4, 64, 128), bf16),
        in_specs=[SMEM, SMEM] + [VMEM] * (2 * segs),
        out_specs=VMEM,
        scratch_shapes=[
            pltpu.VMEM((4 * segs, 64, 128), f32),
            pltpu.VMEM((2 * segs, 64, 128), f32),
            pltpu.VMEM((segs, 8, 128), f32),
            pltpu.SMEM((2 * segs + 4,), jnp.int32),
            pltpu.VMEM((half + 1, 64, 128), f32),
            pltpu.VMEM((half + 1, 64, 128), f32),
            pltpu.VMEM((half, 2, 256, 256), bf16),
            pltpu.VMEM((half, 256, 256), bf16),
            pltpu.VMEM((half + 1, 2, 64, 128), f32),
            pltpu.VMEM((2, 64, 128), f32),
            pltpu.VMEM((half, 2, 256, 256), bf16),
            pltpu.VMEM((half, 256, 256), bf16),
        ],
        compiler_params=pltpu.CompilerParams(vmem_limit_bytes=48 * 2**20),
        name="wire",
    )(place, energy, *own, *other)


def sum_kernel(chips, place_ref, sources_ref, *refs):
    own = refs[:chips]
    other = refs[chips : 2 * chips]
    screened_ref, out_ref, all_ref = refs[2 * chips :]
    chip, core = place_ref[0], place_ref[1]
    for k in range(chips):
        place = jnp.bitwise_xor(chip, k) * cores
        all_ref[place + core] = own[k][...]
        all_ref[place + 1 - core] = other[k][...]
    shifts = screened_ref.shape[0]
    keep = low_lanes(jnp.zeros((64, 128), f32))
    for slot in range(4):
        direct = jnp.zeros((64, 128), f32)
        crossed = jnp.zeros((64, 128), f32)
        for j in range(shifts):
            green = all_ref[sources_ref[0, j], slot].astype(f32)
            weight = screened_ref[j, slot]
            direct = direct + green * weight
            crossed = crossed + green * swapped(weight)
        out_ref[slot] = jnp.where(keep, direct - swapped(direct), crossed + swapped(crossed))


def sum_shifts(place, sources, own, other, screened):
    chips = len(own)

    def kernel(*refs):
        sum_kernel(chips, *refs)

    return pl.pallas_call(
        kernel,
        out_shape=jax.ShapeDtypeStruct(screened.shape[1:], f32),
        in_specs=[SMEM, SMEM] + [VMEM] * (2 * chips + 1),
        out_specs=VMEM,
        scratch_shapes=[pltpu.VMEM((cores * chips,) + screened.shape[1:], bf16)],
        compiler_params=pltpu.CompilerParams(vmem_limit_bytes=48 * 2**20),
        name="sum_shifts",
    )(place, sources, *own, *other, screened)


def flipped_to(x, axis, mask):
    count = lax.axis_size(axis)
    return lax.ppermute(x, axis, [(i, i ^ mask) for i in range(count)])


def body(energies, h_blocks, couplings, shift_real, shift_rate, screened, sources, counts):
    segs = lax.axis_size("seg")
    chips = lax.axis_size("energy") // cores
    seg = lax.axis_index("seg")
    energy = lax.axis_index("energy")
    core, chip = energy % cores, energy // cores
    piece = pack(
        core[None],
        counts,
        h_blocks[0],
        couplings[0],
        shift_real.reshape(2, 128),
        shift_rate.reshape(2, 128),
    )
    own = [piece] + [flipped_to(piece, "seg", k) for k in range(1, segs)]
    other = [flipped_to(x, "energy", 1) for x in own]
    greens = wire(jnp.stack([seg, core]), energies, own, other)
    near = [greens] + [flipped_to(greens, "energy", cores * k) for k in range(1, chips)]
    far = [flipped_to(x, "energy", 1) for x in near]
    out = sum_shifts(jnp.stack([chip, core]), sources, near, far, screened[:, 0])
    return out[None, None]


def solution(mesh):
    in_specs = (
        P("energy"),
        P("seg", None, None, None),
        P("seg", None, None, None),
        P("energy", "seg", None),
        P("energy", "seg", None),
        P(None, "seg", None, None, None),
        P("energy", None),
        P("seg"),
    )
    out_specs = P("energy", "seg", None, None, None)
    return jax.shard_map(body, mesh=mesh, in_specs=in_specs, out_specs=out_specs, check_vma=False)
```

```python
import jax
import jax.numpy as jnp
from jax import lax
from jax.experimental import pallas as pl
from jax.experimental.pallas import tpu as pltpu
from jax.sharding import PartitionSpec as P

broadening = 0.02
cores = 2
f32 = jnp.float32
bf16 = jnp.bfloat16
VMEM = pl.BlockSpec(memory_space=pltpu.VMEM)
SMEM = pl.BlockSpec(memory_space=pltpu.SMEM)


def column(slab, k, lane):
    return jnp.take_along_axis(slab, jnp.where(lane < 64, k, 64 + k), axis=1)


def row(slab, k):
    return jnp.broadcast_to(slab[k : k + 1, :], (8, 128))


def added(parts):
    while len(parts) > 1:
        parts = [a + b for a, b in zip(parts[::2], parts[1::2])]
    return parts[0]


def far_product(whole_r, whole_i, pr, pi, t):
    lane = lax.broadcasted_iota(jnp.int32, (8, 128), 1)
    keep = lane < 64
    source = (lane & 64) + 8 * t + (lane & 7)
    re = jnp.concatenate([jnp.take_along_axis(x, source, axis=1) for x in whole_r], 0)
    im = jnp.concatenate([jnp.take_along_axis(x, source, axis=1) for x in whole_i], 0)
    wide = lax.broadcasted_iota(jnp.int32, re.shape, 1)
    both = jnp.where((wide & 8) > 0, im, re)
    high = both.astype(bf16).astype(f32)
    left = jnp.where(((wide & 63) >> 4) == 1, both - high, high).astype(bf16)
    zero = jnp.zeros((8, 128), f32)
    empty = jnp.zeros((16, 256), bf16)
    right = []
    for kept in (keep, ~keep):
        r, i = jnp.where(kept, pr, zero), jnp.where(kept, pi, zero)
        high, low = split(
            jnp.concatenate([jnp.concatenate([r, i], 1), jnp.concatenate([-i, r], 1)], 0)
        )
        right += [high, high, low, empty]
    out = dot(left, jnp.concatenate(right, 0))
    return out[:, :128], out[:, 128:]


def pair_inverse(mr, mi, beside):
    lane = lax.broadcasted_iota(jnp.int32, (8, 128), 1)
    sub = lax.broadcasted_iota(jnp.int32, (8, 128), 0)
    col = lane & 63
    mr, mi = list(mr), list(mi)
    for t in range(8):
        near = (t + 1) % 8
        far = [(t + d) % 8 for d in range(2, 8)]
        inside = (col >= 8 * t) & (col < 8 * t + 8)
        xr = [column(mr[t], 8 * t + j, lane) for j in range(8)]
        xi = [column(mi[t], 8 * t + j, lane) for j in range(8)]
        cr = [column(mr[near], 8 * t + j, lane) for j in range(8)]
        ci = [column(mi[near], 8 * t + j, lane) for j in range(8)]
        rr = jnp.where(inside, jnp.where(col == sub + 8 * t, 1.0, 0.0), mr[t])
        ri = jnp.where(inside, 0.0, mi[t])
        for k in range(8):
            at = sub == k
            pr, pi = row(xr[k], k), row(xi[k], k)
            q = 1.0 / (pr * pr + pi * pi)
            er, ei = jnp.where(at, -1.0, xr[k]), jnp.where(at, 0.0, xi[k])

            def step(yr, yi):
                ar, ai = row(yr, k), row(yi, k)
                ur, ui = ar * pr + ai * pi, ai * pr - ar * pi
                wr, wi = er * ur - ei * ui, er * ui + ei * ur
                return jnp.where(at, 0.0, yr) - wr * q, jnp.where(at, 0.0, yi) - wi * q

            for j in range(k + 1, 8):
                xr[j], xi[j] = step(xr[j], xi[j])
            rr, ri = step(rr, ri)
        lines = [(row(rr, j), row(ri, j)) for j in range(8)]
        more_r = added([cr[j] * lines[j][0] - ci[j] * lines[j][1] for j in range(8)])
        more_i = added([cr[j] * lines[j][1] + ci[j] * lines[j][0] for j in range(8)])
        mr[near] = jnp.where(inside, 0.0, mr[near]) - more_r
        mi[near] = jnp.where(inside, 0.0, mi[near]) - more_i
        out_r, out_i = far_product([mr[s] for s in far], [mi[s] for s in far], rr, ri, t)
        for n, s in enumerate(far):
            mr[s] = jnp.where(inside, 0.0, mr[s]) - out_r[8 * n : 8 * n + 8]
            mi[s] = jnp.where(inside, 0.0, mi[s]) - out_i[8 * n : 8 * n + 8]
        mr[t], mi[t] = rr, ri
        work = next(beside, None)
        if work is not None:
            work()
    for work in beside:
        work()
    return mr, mi


def slabs(x):
    return [x[8 * s : 8 * s + 8] for s in range(8)]


def invert_pair(zr, zi, beside=()):
    mr, mi = pair_inverse(slabs(zr), slabs(zi), iter(beside))
    return jnp.concatenate(mr, 0), jnp.concatenate(mi, 0)


def low_lanes(x):
    return lax.broadcasted_iota(jnp.int32, x.shape, 1) < 64


def split(x):
    high = x.astype(bf16)
    return high, (x - high.astype(f32)).astype(bf16)


def diagonal(x):
    keep = low_lanes(x)
    zero = jnp.zeros_like(x)
    return jnp.concatenate([jnp.where(keep, x, zero), jnp.where(keep, zero, x)], 0)


def dot(a, b):
    return jnp.dot(a, b, preferred_element_type=f32)


def left_factor(qr, qi):
    rh, rl = split(qr)
    ih, il = split(qi)

    def whole(r, i):
        return jnp.concatenate(
            [jnp.concatenate([r, -i], 1), jnp.concatenate([i, r], 1)], 0
        )

    return jnp.concatenate([whole(rh, ih), whole(rl, il)], 0)


def right_factor(yr, yi):
    def whole(r, i):
        dr, di = diagonal(r), diagonal(i)
        return jnp.concatenate(
            [jnp.concatenate([dr, di], 1), jnp.concatenate([-di, dr], 1)], 0
        )

    rh, rl = split(yr)
    ih, il = split(yi)
    return whole(rh, ih), whole(rl, il)


def times_right(xr, xi, high, low):
    xh, xl = split(jnp.concatenate([xr, xi], 1))
    both = dot(jnp.concatenate([xh, xl], 0), high)
    out = both[:64] + (both[64:] + dot(xh, low))
    return out[:, :128], out[:, 128:]


def times_left(left, xr, xi):
    rh, rl = split(xr)
    ih, il = split(xi)
    right = jnp.concatenate(
        [
            jnp.concatenate([diagonal(rh), diagonal(rl)], 1),
            jnp.concatenate([diagonal(ih), diagonal(il)], 1),
        ],
        0,
    )
    out = dot(left, right)
    out = out[:128, :128] + (out[:128, 128:] + out[128:, :128])
    return out[:64], out[64:]


def swapped(x):
    return pltpu.roll(x, 64, 1)


def packed_pair(one, two):
    lower = lax.broadcasted_iota(jnp.int32, (64, 128), 0) >= (
        lax.broadcasted_iota(jnp.int32, (64, 128), 1) & 63
    )
    left = jnp.where(lower, one, swapped(one))
    right = jnp.where(lower, swapped(two), two)
    return jnp.where(low_lanes(one), left, right)


def pack_kernel(
    counts_ref, shifts_ref, rates_ref, hams_ref, links_ref, out_ref
):
    first = 2 * (lax.axis_index("energy") & 1)
    out_ref[0:64] = links_ref[first]
    out_ref[64:128] = links_ref[first + 1]
    out_ref[128:192] = packed_pair(hams_ref[first], hams_ref[first + 1])
    out_ref[192:194] = shifts_ref[...]
    out_ref[194:196] = rates_ref[...]
    out_ref[196:200] = jnp.broadcast_to(counts_ref[...].astype(f32), (4, 128))


def pack(*arrays):
    return pl.pallas_call(
        pack_kernel,
        out_shape=jax.ShapeDtypeStruct((200, 128), f32),
        in_specs=[VMEM] * len(arrays),
        out_specs=VMEM,
        name="pack",
    )(*arrays)


def settle_kernel(energies_ref, in_ref, out_ref):
    out_ref[0:192] = in_ref[0:192]
    last = lax.broadcasted_iota(jnp.int32, (8, 128), 0) >= 6
    out_ref[192:200] = jnp.where(last, energies_ref[0], in_ref[192:200])


def settle(energies, piece):
    return pl.pallas_call(
        settle_kernel,
        out_shape=jax.ShapeDtypeStruct(piece.shape, f32),
        in_specs=[SMEM, VMEM],
        out_specs=VMEM,
        compiler_params=pltpu.CompilerParams(vmem_limit_bytes=4 * 2**20),
        name="settle",
    )(energies, piece)


def wire_kernel(segs, *refs):
    own = refs[:segs]
    other = refs[segs : 2 * segs]
    out_ref = refs[2 * segs]
    (u_ref, h_ref, m_ref, at_ref, ar_ref, ai_ref, yright_ref, yleft_ref, g_ref, s_ref, k_ref, t_ref) = (
        refs[2 * segs + 1 :]
    )
    blocks = 2 * segs
    half = segs
    place, core = lax.axis_index("seg"), lax.axis_index("energy") & 1

    for k in range(segs):
        seg = jnp.bitwise_xor(place, k)
        for c, ref in ((core, own[k]), (1 - core, other[k])):
            u_ref[4 * seg + 2 * c] = ref[0:64]
            u_ref[4 * seg + 2 * c + 1] = ref[64:128]
            h_ref[2 * seg + c] = ref[128:192]
        m_ref[seg] = own[k][192:200]
    energy = own[0][198:199]

    start = jnp.int32(0)
    first, used = jnp.int32(0), jnp.int32(0)
    for seg in range(segs):
        count = jnp.max(m_ref[seg, 4:5, :]).astype(jnp.int32)
        for k in range(4):
            at_ref[start + k] = 4 * seg + k
        first = jnp.where(seg == place, start, first)
        used = jnp.where(seg == place, count, used)
        start = start + count

    keep = low_lanes(jnp.zeros((64, 128), f32))
    rows = lax.broadcasted_iota(jnp.int32, (64, 128), 0)
    cols = lax.broadcasted_iota(jnp.int32, (64, 128), 1) & 63

    def prepare_block(i, carry):
        one, two = at_ref[i], at_ref[blocks - 1 - i]
        odd_one, odd_two = one & 1, two & 1
        raw_one, raw_two = h_ref[one >> 1], h_ref[two >> 1]
        one_low = pltpu.roll(raw_one, 64 * odd_one, 1)
        two_low = pltpu.roll(raw_two, 64 * odd_two, 1)
        two_high = pltpu.roll(raw_two, 64 * (1 - odd_two), 1)
        packed = jnp.where(keep, one_low, two_high)
        flipped = jnp.concatenate([one_low, two_low], 0).T[:64]
        real = jnp.where(rows >= cols, packed, flipped)
        imag = jnp.where(rows < cols, packed, jnp.where(rows > cols, -flipped, 0.0))
        extra = []
        for base in (0, 2):
            line_one = m_ref[one >> 2, pl.ds(base + ((one >> 1) & 1), 1), :]
            line_two = m_ref[two >> 2, pl.ds(base + ((two >> 1) & 1), 1), :]
            line_one = pltpu.roll(jnp.broadcast_to(line_one, (8, 128)), 64 * odd_one, 1)
            line_two = pltpu.roll(jnp.broadcast_to(line_two, (8, 128)), 64 * (1 - odd_two), 1)
            line = jnp.where(keep[:8], line_one, line_two)
            extra.append(jnp.broadcast_to(line[:1], (64, 128)))
        on = rows == cols
        ar_ref[i] = jnp.where(on, energy - extra[0], 0.0) - real
        ai_ref[i] = jnp.where(on, broadening + extra[1], 0.0) - imag
        return carry

    def prepare_link(i, carry):
        one, two = u_ref[at_ref[i]], u_ref[at_ref[blocks - i]]
        flat_re = jnp.where(keep, one, swapped(two))
        flat_im = jnp.where(keep, swapped(one), two)
        turned = jnp.concatenate([one, two], 0).T
        turned_re, turned_im = turned[:64], -turned[64:]
        high, low = right_factor(
            jnp.where(keep, flat_re, turned_re), jnp.where(keep, flat_im, turned_im)
        )
        yright_ref[i - 1, 0] = high
        yright_ref[i - 1, 1] = low
        yleft_ref[i - 1] = left_factor(
            jnp.where(keep, turned_re, flat_re), jnp.where(keep, turned_im, flat_im)
        )
        return carry

    def long_wire():
        lax.fori_loop(0, half, prepare_block, 0)
        lax.fori_loop(1, half + 1, prepare_link, 0)

        s_ref[...] = jnp.zeros_like(s_ref)

        def inward(i, carry):
            fr = ar_ref[i] - s_ref[0]
            fi = ai_ref[i] - s_ref[1]
            gr, gi = invert_pair(fr, fi)
            g_ref[i, 0] = gr
            g_ref[i, 1] = gi

            @pl.when(i < half)
            def _():
                tr, ti = times_right(gr, gi, yright_ref[i, 0], yright_ref[i, 1])
                t_ref[i] = left_factor(tr, ti)
                sr, si = times_left(yleft_ref[i], tr, ti)
                kr, ki = times_left(yleft_ref[i], gr, gi)
                high, low = right_factor(kr, ki)
                k_ref[i, 0] = high
                k_ref[i, 1] = low
                s_ref[0] = sr
                s_ref[1] = si

            @pl.when(i == half - 1)
            def _():
                s_ref[0] = swapped(s_ref[0])
                s_ref[1] = swapped(s_ref[1])
                ar_ref[half] = fr
                ai_ref[half] = fi

            return carry

        lax.fori_loop(0, half + 1, inward, 0)

        g_ref[half - 1] = g_ref[half]

        def outward(step, carry):
            i = half - 2 - step
            zr, zi = times_right(g_ref[i + 1, 0], g_ref[i + 1, 1], k_ref[i, 0], k_ref[i, 1])
            wr, wi = times_left(t_ref[i], zr, zi)
            g_ref[i, 0] = g_ref[i, 0] + wr
            g_ref[i, 1] = g_ref[i, 1] + wi
            return carry

        lax.fori_loop(0, half - 1, outward, 0)

    def short_wire():
        last = half - 2
        g, t, k = [None] * half, [None] * half, [None] * half
        base, left, right = [None] * half, [None] * half, [None] * half

        def do_block(i):
            return lambda: prepare_block(i, 0)

        def do_link(i):
            return lambda: prepare_link(i, 0)

        def do_k(i):
            def run():
                k[i] = times_left(yleft_ref[i], *g[i])
                high, low = right_factor(*k[i])
                k_ref[i, 0] = high
                k_ref[i, 1] = low
                if i == last:
                    base[i], left[i], right[i] = g[i], t[i], k[i]

            return run

        def do_outer(i):
            def one():
                base[i] = times_left(t_ref[i], *base[i + 1])

            def two():
                more = times_right(*base[i], k_ref[i, 0], k_ref[i, 1])
                base[i] = (g[i][0] + more[0], g[i][1] + more[1])

            def three():
                left[i] = times_left(t_ref[i], *left[i + 1])
                t_ref[i] = left_factor(*left[i])

            def four():
                right[i] = times_right(*right[i + 1], k_ref[i, 0], k_ref[i, 1])
                high, low = right_factor(*right[i])
                k_ref[i, 0] = high
                k_ref[i, 1] = low

            return [one, two, three, four]

        beside = [[] for _ in range(half + 1)]
        beside[0] = [do_link(1), do_block(1)]
        for i in range(2, half):
            beside[0] += [do_block(i), do_link(i)]
        beside[0] += [do_link(half)]
        for i in range(half - 1):
            beside[i + 1] += [do_k(i)]
        for n, i in enumerate(range(last - 1, -1, -1)):
            beside[min(half - 1 + n, half)] += do_outer(i)

        prepare_block(0, 0)
        sr = si = None
        for i in range(half + 1):
            if i == 0:
                fr, fi = ar_ref[0], ai_ref[0]
            elif i < half:
                fr, fi = ar_ref[i] - sr, ai_ref[i] - si
            else:
                fr, fi = fr - swapped(sr), fi - swapped(si)
            zr, zi = invert_pair(fr, fi, beside[i])
            if i < half:
                g[i] = (zr, zi)
                t[i] = times_right(zr, zi, yright_ref[i, 0], yright_ref[i, 1])
                sr, si = times_left(yleft_ref[i], *t[i])
                if i < half - 1:
                    t_ref[i] = left_factor(*t[i])
        g_ref[half - 1, 0] = zr
        g_ref[half - 1, 1] = zi
        for i in range(half - 1):
            more = times_right(zr, zi, k_ref[i, 0], k_ref[i, 1])
            more = times_left(t_ref[i], *more)
            g_ref[i, 0] = base[i][0] + more[0]
            g_ref[i, 1] = base[i][1] + more[1]

    if half in (3, 4, 5):
        short_wire()
    else:
        long_wire()

    for k in range(4):
        block = jnp.minimum(first + k, blocks - 1)
        right = (block >= half).astype(jnp.int32)
        i = jnp.where(block >= half, blocks - 1 - block, block)
        re = pltpu.roll(g_ref[i, 0], 64 * right, 1)
        im = pltpu.roll(g_ref[i, 1], 64 * (1 - right), 1)
        live = (k < used).astype(f32)
        out_ref[k] = (jnp.where(keep, re, im) * live).astype(bf16)


def wire(own, other):
    segs = len(own)
    half = segs

    def kernel(*refs):
        wire_kernel(segs, *refs)

    return pl.pallas_call(
        kernel,
        out_shape=jax.ShapeDtypeStruct((4, 64, 128), bf16),
        in_specs=[VMEM] * (2 * segs),
        out_specs=VMEM,
        scratch_shapes=[
            pltpu.VMEM((4 * segs, 64, 128), f32),
            pltpu.VMEM((2 * segs, 64, 128), f32),
            pltpu.VMEM((segs, 8, 128), f32),
            pltpu.SMEM((2 * segs + 4,), jnp.int32),
            pltpu.VMEM((half + 1, 64, 128), f32),
            pltpu.VMEM((half + 1, 64, 128), f32),
            pltpu.VMEM((half, 2, 256, 256), bf16),
            pltpu.VMEM((half, 256, 256), bf16),
            pltpu.VMEM((half + 1, 2, 64, 128), f32),
            pltpu.VMEM((2, 64, 128), f32),
            pltpu.VMEM((half, 2, 256, 256), bf16),
            pltpu.VMEM((half, 256, 256), bf16),
        ],
        compiler_params=pltpu.CompilerParams(vmem_limit_bytes=(8 + 2 * segs) * 2**20),
        name="wire",
    )(*own, *other)


def sum_kernel(chips, sources_ref, *refs):
    own = refs[:chips]
    other = refs[chips : 2 * chips]
    screened_ref, out_ref, all_ref = refs[2 * chips :]
    chip, core = lax.axis_index("energy") >> 1, lax.axis_index("energy") & 1
    for k in range(chips):
        place = jnp.bitwise_xor(chip, k) * cores
        all_ref[place + core] = own[k][...]
        all_ref[place + 1 - core] = other[k][...]
    shifts = screened_ref.shape[0]
    keep = low_lanes(jnp.zeros((64, 128), f32))
    for slot in range(4):
        direct = jnp.zeros((64, 128), f32)
        crossed = jnp.zeros((64, 128), f32)
        for j in range(shifts):
            green = all_ref[sources_ref[0, j], slot].astype(f32)
            weight = screened_ref[j, slot]
            direct = direct + green * weight
            crossed = crossed + green * swapped(weight)
        out_ref[slot] = jnp.where(keep, direct - swapped(direct), crossed + swapped(crossed))


def sum_shifts(sources, own, other, screened):
    chips = len(own)

    def kernel(*refs):
        sum_kernel(chips, *refs)

    return pl.pallas_call(
        kernel,
        out_shape=jax.ShapeDtypeStruct(screened.shape[1:], f32),
        in_specs=[SMEM] + [VMEM] * (2 * chips + 1),
        out_specs=VMEM,
        scratch_shapes=[pltpu.VMEM((cores * chips,) + screened.shape[1:], bf16)],
        compiler_params=pltpu.CompilerParams(vmem_limit_bytes=(4 + 2 * chips) * 2**20),
        name="sum_shifts",
    )(sources, *own, *other, screened)


def flipped_to(x, axis, mask):
    count = lax.axis_size(axis)
    return lax.ppermute(x, axis, [(i, i ^ mask) for i in range(count)])


def body(energies, h_blocks, couplings, shift_real, shift_rate, screened, sources, counts):
    segs = lax.axis_size("seg")
    chips = lax.axis_size("energy") // cores
    first = lax.axis_index("energy") % cores == 0
    hams, links = h_blocks[0], couplings[0]
    one = jnp.where(first, hams[0], hams[2])
    two = jnp.where(first, hams[1], hams[3])
    lower = jnp.arange(64)[:, None] >= jnp.arange(64)[None, :]
    packed = jnp.concatenate(
        [jnp.where(lower, one[:, :64], one[:, 64:]), jnp.where(lower, two[:, :64], two[:, 64:])], 1
    )
    piece = jnp.concatenate(
        [
            jnp.where(first, links[0], links[2]),
            jnp.where(first, links[1], links[3]),
            packed,
            shift_real.reshape(2, 128),
            shift_rate.reshape(2, 128),
            jnp.broadcast_to(counts.astype(f32)[:, None], (4, 128)),
        ],
        0,
    )
    sent = [flipped_to(piece, "seg", k) for k in range(1, segs)]
    own = [settle(energies, piece)] + sent
    other = [flipped_to(x, "energy", 1) for x in [piece] + sent]
    greens = wire(own, other)
    near = [greens] + [flipped_to(greens, "energy", cores * k) for k in range(1, chips)]
    far = [flipped_to(x, "energy", 1) for x in near]
    return sum_shifts(sources, near, far, screened[:, 0])[None, None]


def solution(mesh):
    in_specs = (
        P("energy"),
        P("seg", None, None, None),
        P("seg", None, None, None),
        P("energy", "seg", None),
        P("energy", "seg", None),
        P(None, "seg", None, None, None),
        P("energy", None),
        P("seg"),
    )
    out_specs = P("energy", "seg", None, None, None)
    return jax.shard_map(body, mesh=mesh, in_specs=in_specs, out_specs=out_specs, check_vma=False)
```

```python
import jax
import jax.numpy as jnp
from jax import lax
from jax.experimental import pallas as pl
from jax.experimental.pallas import tpu as pltpu
from jax.sharding import PartitionSpec as P

broadening = 0.02
cores = 2
f32 = jnp.float32
bf16 = jnp.bfloat16
VMEM = pl.BlockSpec(memory_space=pltpu.VMEM)
SMEM = pl.BlockSpec(memory_space=pltpu.SMEM)


def column(slab, k, lane):
    return jnp.take_along_axis(slab, jnp.where(lane < 64, k, 64 + k), axis=1)


def row(slab, k):
    return jnp.broadcast_to(slab[k : k + 1, :], (8, 128))


def added(parts):
    while len(parts) > 1:
        parts = [a + b for a, b in zip(parts[::2], parts[1::2])]
    return parts[0]


def far_product(whole_r, whole_i, pr, pi, t):
    lane = lax.broadcasted_iota(jnp.int32, (8, 128), 1)
    keep = lane < 64
    source = (lane & 64) + 8 * t + (lane & 7)
    re = jnp.concatenate([jnp.take_along_axis(x, source, axis=1) for x in whole_r], 0)
    im = jnp.concatenate([jnp.take_along_axis(x, source, axis=1) for x in whole_i], 0)
    wide = lax.broadcasted_iota(jnp.int32, re.shape, 1)
    both = jnp.where((wide & 8) > 0, im, re)
    high = both.astype(bf16).astype(f32)
    left = jnp.where(((wide & 63) >> 4) == 1, both - high, high).astype(bf16)
    zero = jnp.zeros((8, 128), f32)
    empty = jnp.zeros((16, 256), bf16)
    right = []
    for kept in (keep, ~keep):
        r, i = jnp.where(kept, pr, zero), jnp.where(kept, pi, zero)
        high, low = split(
            jnp.concatenate([jnp.concatenate([r, i], 1), jnp.concatenate([-i, r], 1)], 0)
        )
        right += [high, high, low, empty]
    out = dot(left, jnp.concatenate(right, 0))
    return out[:, :128], out[:, 128:]


def panels(mr, mi):
    lane = lax.broadcasted_iota(jnp.int32, (8, 128), 1)
    sub = lax.broadcasted_iota(jnp.int32, (8, 128), 0)
    col = lane & 63
    for t in range(8):
        near = (t + 1) % 8
        far = [(t + d) % 8 for d in range(2, 8)]
        inside = (col >= 8 * t) & (col < 8 * t + 8)
        xr = [column(mr[t], 8 * t + j, lane) for j in range(8)]
        xi = [column(mi[t], 8 * t + j, lane) for j in range(8)]
        cr = [column(mr[near], 8 * t + j, lane) for j in range(8)]
        ci = [column(mi[near], 8 * t + j, lane) for j in range(8)]
        rr = jnp.where(inside, jnp.where(col == sub + 8 * t, 1.0, 0.0), mr[t])
        ri = jnp.where(inside, 0.0, mi[t])
        vr, vi = jnp.ones((8, 128), f32), jnp.zeros((8, 128), f32)
        for k in range(8):
            at = sub == k
            pr, pi = row(xr[k], k), row(xi[k], k)
            q = 1.0 / (pr * pr + pi * pi)
            er, ei = jnp.where(at, 0.0, xr[k]), jnp.where(at, 0.0, xi[k])
            fr, fi = er * pr + ei * pi, ei * pr - er * pi
            vr, vi = jnp.where(at, pr * q, vr), jnp.where(at, -(pi * q), vi)

            def step(yr, yi):
                ar, ai = row(yr, k), row(yi, k)
                wr, wi = fr * ar - fi * ai, fr * ai + fi * ar
                return yr - wr * q, yi - wi * q

            for j in range(k + 1, 8):
                xr[j], xi[j] = step(xr[j], xi[j])
            rr, ri = step(rr, ri)
        rr, ri = rr * vr - ri * vi, rr * vi + ri * vr
        lines = [(row(rr, j), row(ri, j)) for j in range(8)]
        more_r = added([cr[j] * lines[j][0] - ci[j] * lines[j][1] for j in range(8)])
        more_i = added([cr[j] * lines[j][1] + ci[j] * lines[j][0] for j in range(8)])
        mr[near] = jnp.where(inside, 0.0, mr[near]) - more_r
        mi[near] = jnp.where(inside, 0.0, mi[near]) - more_i
        out_r, out_i = far_product([mr[s] for s in far], [mi[s] for s in far], rr, ri, t)
        for n, s in enumerate(far):
            mr[s] = jnp.where(inside, 0.0, mr[s]) - out_r[8 * n : 8 * n + 8]
            mi[s] = jnp.where(inside, 0.0, mi[s]) - out_i[8 * n : 8 * n + 8]
        mr[t], mi[t] = rr, ri
        yield


def slabs(x):
    return [x[8 * s : 8 * s + 8] for s in range(8)]


def invert_pairs(pairs, beside=()):
    beside = iter(beside)
    held = [(slabs(zr), slabs(zi)) for zr, zi in pairs]
    for _ in zip(*[panels(mr, mi) for mr, mi in held]):
        work = next(beside, None)
        if work is not None:
            work()
    for work in beside:
        work()
    return [(jnp.concatenate(mr, 0), jnp.concatenate(mi, 0)) for mr, mi in held]


def low_lanes(x):
    return lax.broadcasted_iota(jnp.int32, x.shape, 1) < 64


def split(x):
    high = x.astype(bf16)
    return high, (x - high.astype(f32)).astype(bf16)


def diagonal(x):
    keep = low_lanes(x)
    zero = jnp.zeros_like(x)
    return jnp.concatenate([jnp.where(keep, x, zero), jnp.where(keep, zero, x)], 0)


def dot(a, b):
    return jnp.dot(a, b, preferred_element_type=f32)


def left_factor(qr, qi):
    rh, rl = split(qr)
    ih, il = split(qi)

    def whole(r, i):
        return jnp.concatenate(
            [jnp.concatenate([r, -i], 1), jnp.concatenate([i, r], 1)], 0
        )

    return jnp.concatenate([whole(rh, ih), whole(rl, il)], 0)


def right_factor(yr, yi):
    def whole(r, i):
        dr, di = diagonal(r), diagonal(i)
        return jnp.concatenate(
            [jnp.concatenate([dr, di], 1), jnp.concatenate([-di, dr], 1)], 0
        )

    rh, rl = split(yr)
    ih, il = split(yi)
    return whole(rh, ih), whole(rl, il)


def times_right(xr, xi, high, low):
    xh, xl = split(jnp.concatenate([xr, xi], 1))
    both = dot(jnp.concatenate([xh, xl], 0), high)
    out = both[:64] + (both[64:] + dot(xh, low))
    return out[:, :128], out[:, 128:]


def times_left(left, xr, xi):
    rh, rl = split(xr)
    ih, il = split(xi)
    right = jnp.concatenate(
        [
            jnp.concatenate([diagonal(rh), diagonal(rl)], 1),
            jnp.concatenate([diagonal(ih), diagonal(il)], 1),
        ],
        0,
    )
    out = dot(left, right)
    out = out[:128, :128] + (out[:128, 128:] + out[128:, :128])
    return out[:64], out[64:]


def swapped(x):
    return pltpu.roll(x, 64, 1)


def packed_pair(one, two):
    lower = lax.broadcasted_iota(jnp.int32, (64, 128), 0) >= (
        lax.broadcasted_iota(jnp.int32, (64, 128), 1) & 63
    )
    left = jnp.where(lower, one, swapped(one))
    right = jnp.where(lower, swapped(two), two)
    return jnp.where(low_lanes(one), left, right)


def pack_kernel(
    counts_ref, shifts_ref, rates_ref, hams_ref, links_ref, out_ref
):
    first = 2 * (lax.axis_index("energy") & 1)
    out_ref[0:64] = links_ref[first]
    out_ref[64:128] = links_ref[first + 1]
    out_ref[128:192] = packed_pair(hams_ref[first], hams_ref[first + 1])
    out_ref[192:194] = shifts_ref[...]
    out_ref[194:196] = rates_ref[...]
    out_ref[196:200] = jnp.broadcast_to(counts_ref[...].astype(f32), (4, 128))


def pack(*arrays):
    return pl.pallas_call(
        pack_kernel,
        out_shape=jax.ShapeDtypeStruct((200, 128), f32),
        in_specs=[VMEM] * len(arrays),
        out_specs=VMEM,
        name="pack",
    )(*arrays)


def settle_kernel(energies_ref, in_ref, out_ref):
    out_ref[0:192] = in_ref[0:192]
    last = lax.broadcasted_iota(jnp.int32, (8, 128), 0) >= 6
    out_ref[192:200] = jnp.where(last, energies_ref[0], in_ref[192:200])


def settle(energies, piece):
    return pl.pallas_call(
        settle_kernel,
        out_shape=jax.ShapeDtypeStruct(piece.shape, f32),
        in_specs=[SMEM, VMEM],
        out_specs=VMEM,
        compiler_params=pltpu.CompilerParams(vmem_limit_bytes=4 * 2**20),
        name="settle",
    )(energies, piece)


def wire_kernel(segs, *refs):
    own = refs[:segs]
    other = refs[segs : 2 * segs]
    out_ref = refs[2 * segs]
    (u_ref, h_ref, m_ref, at_ref, ar_ref, ai_ref, yright_ref, yleft_ref, g_ref, s_ref, k_ref, t_ref) = (
        refs[2 * segs + 1 :]
    )
    blocks = 2 * segs
    half = segs
    place, core = lax.axis_index("seg"), lax.axis_index("energy") & 1

    for k in range(segs):
        seg = jnp.bitwise_xor(place, k)
        for c, ref in ((core, own[k]), (1 - core, other[k])):
            u_ref[4 * seg + 2 * c] = ref[0:64]
            u_ref[4 * seg + 2 * c + 1] = ref[64:128]
            h_ref[2 * seg + c] = ref[128:192]
        m_ref[seg] = own[k][192:200]
    energy = own[0][198:199]

    start = jnp.int32(0)
    first, used = jnp.int32(0), jnp.int32(0)
    for seg in range(segs):
        count = jnp.max(m_ref[seg, 4:5, :]).astype(jnp.int32)
        for k in range(4):
            at_ref[start + k] = 4 * seg + k
        first = jnp.where(seg == place, start, first)
        used = jnp.where(seg == place, count, used)
        start = start + count

    keep = low_lanes(jnp.zeros((64, 128), f32))
    rows = lax.broadcasted_iota(jnp.int32, (64, 128), 0)
    cols = lax.broadcasted_iota(jnp.int32, (64, 128), 1) & 63

    def prepare_block(i, carry):
        one, two = at_ref[i], at_ref[blocks - 1 - i]
        odd_one, odd_two = one & 1, two & 1
        raw_one, raw_two = h_ref[one >> 1], h_ref[two >> 1]
        one_low = pltpu.roll(raw_one, 64 * odd_one, 1)
        two_low = pltpu.roll(raw_two, 64 * odd_two, 1)
        two_high = pltpu.roll(raw_two, 64 * (1 - odd_two), 1)
        packed = jnp.where(keep, one_low, two_high)
        flipped = jnp.concatenate([one_low, two_low], 0).T[:64]
        real = jnp.where(rows >= cols, packed, flipped)
        imag = jnp.where(rows < cols, packed, jnp.where(rows > cols, -flipped, 0.0))
        extra = []
        for base in (0, 2):
            line_one = m_ref[one >> 2, pl.ds(base + ((one >> 1) & 1), 1), :]
            line_two = m_ref[two >> 2, pl.ds(base + ((two >> 1) & 1), 1), :]
            line_one = pltpu.roll(jnp.broadcast_to(line_one, (8, 128)), 64 * odd_one, 1)
            line_two = pltpu.roll(jnp.broadcast_to(line_two, (8, 128)), 64 * (1 - odd_two), 1)
            line = jnp.where(keep[:8], line_one, line_two)
            extra.append(jnp.broadcast_to(line[:1], (64, 128)))
        on = rows == cols
        ar_ref[i] = jnp.where(on, energy - extra[0], 0.0) - real
        ai_ref[i] = jnp.where(on, broadening + extra[1], 0.0) - imag
        return carry

    def prepare_link(i, carry):
        one, two = u_ref[at_ref[i]], u_ref[at_ref[blocks - i]]
        flat_re = jnp.where(keep, one, swapped(two))
        flat_im = jnp.where(keep, swapped(one), two)
        turned = jnp.concatenate([one, two], 0).T
        turned_re, turned_im = turned[:64], -turned[64:]
        y = jnp.where(keep, flat_re, turned_re), jnp.where(keep, flat_im, turned_im)
        y_adjoint = jnp.where(keep, turned_re, flat_re), jnp.where(keep, turned_im, flat_im)
        high, low = right_factor(*y)
        yright_ref[i - 1, 0] = high
        yright_ref[i - 1, 1] = low
        yleft_ref[i - 1] = left_factor(*y_adjoint)
        return y, y_adjoint

    def long_wire():
        lax.fori_loop(0, half, prepare_block, 0)
        lax.fori_loop(1, half + 1, lambda i, carry: prepare_link(i, carry) and carry, 0)

        s_ref[...] = jnp.zeros_like(s_ref)

        def inward(i, carry):
            fr = ar_ref[i] - s_ref[0]
            fi = ai_ref[i] - s_ref[1]
            ((gr, gi),) = invert_pairs([(fr, fi)])
            g_ref[i, 0] = gr
            g_ref[i, 1] = gi

            @pl.when(i < half)
            def _():
                tr, ti = times_right(gr, gi, yright_ref[i, 0], yright_ref[i, 1])
                t_ref[i] = left_factor(tr, ti)
                sr, si = times_left(yleft_ref[i], tr, ti)
                kr, ki = times_left(yleft_ref[i], gr, gi)
                high, low = right_factor(kr, ki)
                k_ref[i, 0] = high
                k_ref[i, 1] = low
                s_ref[0] = sr
                s_ref[1] = si

            @pl.when(i == half - 1)
            def _():
                s_ref[0] = swapped(s_ref[0])
                s_ref[1] = swapped(s_ref[1])
                ar_ref[half] = fr
                ai_ref[half] = fi

            return carry

        lax.fori_loop(0, half + 1, inward, 0)

        g_ref[half - 1] = g_ref[half]

        def outward(step, carry):
            i = half - 2 - step
            zr, zi = times_right(g_ref[i + 1, 0], g_ref[i + 1, 1], k_ref[i, 0], k_ref[i, 1])
            wr, wi = times_left(t_ref[i], zr, zi)
            g_ref[i, 0] = g_ref[i, 0] + wr
            g_ref[i, 1] = g_ref[i, 1] + wi
            return carry

        lax.fori_loop(0, half - 1, outward, 0)

    def wire_of_eight():
        v = {}

        def plus(x, y):
            return x[0] + y[0], x[1] + y[1]

        def minus(x, y):
            return x[0] - y[0], x[1] - y[1]

        def block(i):
            return ar_ref[i], ai_ref[i]

        def by_y(x, i):
            return times_right(*x, yright_ref[i - 1, 0], yright_ref[i - 1, 1])

        def adjoint_y_by(i, x):
            return times_left(yleft_ref[i - 1], *x)

        def do(step, *args):
            return lambda: step(*args)

        def link_two():
            y, y_adjoint = prepare_link(2, 0)
            v["y2_left"] = left_factor(*y)
            v["y2_adjoint_right"] = right_factor(*y_adjoint)

        def hold(name, product, *names):
            def run():
                v[name] = product(*[v[x] for x in names])

            return run

        def left_form(x):
            return left_factor(*x)

        def right_form(x):
            return right_factor(*x)

        def left_times(left, x):
            return times_left(left, *x)

        def times_right_form(x, right):
            return times_right(*x, *right)

        prepare_block(0, 0)
        prepare_block(2, 0)
        v["g0"], v["g2"] = invert_pairs(
            [block(0), block(2)],
            [
                do(prepare_link, 1, 0),
                link_two,
                do(prepare_block, 1, 0),
                do(prepare_link, 3, 0),
                do(prepare_block, 3, 0),
                do(prepare_link, 4, 0),
            ],
        )
        v["t0"] = by_y(v["g0"], 1)
        v["p_"] = left_times(v["y2_left"], v["g2"])
        first_one = minus(block(1), adjoint_y_by(1, v["t0"]))
        first_one = minus(first_one, times_right_form(v["p_"], v["y2_adjoint_right"]))

        def third():
            v["q_"] = adjoint_y_by(3, v["g2"])

        def fourth():
            v["f3"] = minus(block(3), by_y(v["q_"], 3))

        def w13():
            v["w13"] = right_form(by_y(v["p_"], 3))

        def w31():
            v["w31"] = left_form(times_right_form(v["q_"], v["y2_adjoint_right"]))

        def k0():
            v["k0"] = right_form(adjoint_y_by(1, v["g0"]))

        def q():
            v["q"] = by_y(v["g2"], 3)

        def p():
            v["p"] = left_form(times_right_form(v["g2"], v["y2_adjoint_right"]))

        def forms():
            v["t0_left"] = left_form(v["t0"])
            v["p_right"] = right_form(v["p_"])

        (v["g1"],) = invert_pairs([first_one], [third, w13, w31, fourth, k0, q, p, forms])
        v["m"] = times_right_form(v["g1"], v["w13"])
        f3 = minus(v["f3"], left_times(v["w31"], v["m"]))

        def base_zero():
            v["base0"] = plus(v["g0"], times_right_form(v["t0_g1"], v["k0"]))

        def base_two():
            v["base2"] = plus(v["g2"], times_right_form(v["p_g1"], v["p_right"]))

        def left_two():
            v["left2"] = left_form(plus(left_times(v["p"], v["m"]), v["q"]))

        def right_two():
            v["right2"] = right_form(plus(times_right_form(v["n"], v["p_right"]), v["q_"]))

        def left_zero():
            v["left0"] = left_form(left_times(v["t0_left"], v["m"]))

        def right_zero():
            v["right0"] = right_form(times_right_form(v["n"], v["k0"]))

        def ends():
            v["left1"] = left_form(v["m"])
            v["right1"] = right_form(v["n"])

        (g3,) = invert_pairs(
            [f3],
            [
                hold("n", left_times, "w31", "g1"),
                hold("t0_g1", left_times, "t0_left", "g1"),
                hold("p_g1", left_times, "p", "g1"),
                base_zero,
                base_two,
                left_two,
                right_two,
                ends,
            ],
        )
        across = adjoint_y_by(4, by_y(g3, 4))
        middle = minus(f3, (swapped(across[0]), swapped(across[1])))
        (g_middle,) = invert_pairs([middle], [left_zero, right_zero])
        g_ref[3, 0], g_ref[3, 1] = g_middle
        for i, base in ((0, "base0"), (1, "g1"), (2, "base2")):
            more = times_right_form(g_middle, v["right" + str(i)])
            g_ref[i, 0], g_ref[i, 1] = plus(v[base], left_times(v["left" + str(i)], more))

    if half == 4:
        wire_of_eight()
    else:
        long_wire()

    for k in range(4):
        block = jnp.minimum(first + k, blocks - 1)
        right = (block >= half).astype(jnp.int32)
        i = jnp.where(block >= half, blocks - 1 - block, block)
        re = pltpu.roll(g_ref[i, 0], 64 * right, 1)
        im = pltpu.roll(g_ref[i, 1], 64 * (1 - right), 1)
        live = (k < used).astype(f32)
        out_ref[k] = (jnp.where(keep, re, im) * live).astype(bf16)


def wire(own, other):
    segs = len(own)
    half = segs

    def kernel(*refs):
        wire_kernel(segs, *refs)

    return pl.pallas_call(
        kernel,
        out_shape=jax.ShapeDtypeStruct((4, 64, 128), bf16),
        in_specs=[VMEM] * (2 * segs),
        out_specs=VMEM,
        scratch_shapes=[
            pltpu.VMEM((4 * segs, 64, 128), f32),
            pltpu.VMEM((2 * segs, 64, 128), f32),
            pltpu.VMEM((segs, 8, 128), f32),
            pltpu.SMEM((2 * segs + 4,), jnp.int32),
            pltpu.VMEM((half + 1, 64, 128), f32),
            pltpu.VMEM((half + 1, 64, 128), f32),
            pltpu.VMEM((half, 2, 256, 256), bf16),
            pltpu.VMEM((half, 256, 256), bf16),
            pltpu.VMEM((half + 1, 2, 64, 128), f32),
            pltpu.VMEM((2, 64, 128), f32),
            pltpu.VMEM((half, 2, 256, 256), bf16),
            pltpu.VMEM((half, 256, 256), bf16),
        ],
        compiler_params=pltpu.CompilerParams(vmem_limit_bytes=(8 + 2 * segs) * 2**20),
        name="wire",
    )(*own, *other)


def sum_kernel(chips, sources_ref, *refs):
    own = refs[:chips]
    other = refs[chips : 2 * chips]
    screened_ref, out_ref, all_ref = refs[2 * chips :]
    chip, core = lax.axis_index("energy") >> 1, lax.axis_index("energy") & 1
    for k in range(chips):
        place = jnp.bitwise_xor(chip, k) * cores
        all_ref[place + core] = own[k][...]
        all_ref[place + 1 - core] = other[k][...]
    shifts = screened_ref.shape[0]
    keep = low_lanes(jnp.zeros((64, 128), f32))
    for slot in range(4):
        direct = jnp.zeros((64, 128), f32)
        crossed = jnp.zeros((64, 128), f32)
        for j in range(shifts):
            green = all_ref[sources_ref[0, j], slot].astype(f32)
            weight = screened_ref[j, slot]
            direct = direct + green * weight
            crossed = crossed + green * swapped(weight)
        out_ref[slot] = jnp.where(keep, direct - swapped(direct), crossed + swapped(crossed))


def sum_shifts(sources, own, other, screened):
    chips = len(own)

    def kernel(*refs):
        sum_kernel(chips, *refs)

    return pl.pallas_call(
        kernel,
        out_shape=jax.ShapeDtypeStruct(screened.shape[1:], f32),
        in_specs=[SMEM] + [VMEM] * (2 * chips + 1),
        out_specs=VMEM,
        scratch_shapes=[pltpu.VMEM((cores * chips,) + screened.shape[1:], bf16)],
        compiler_params=pltpu.CompilerParams(vmem_limit_bytes=(4 + 2 * chips) * 2**20),
        name="sum_shifts",
    )(sources, *own, *other, screened)


def flipped_to(x, axis, mask):
    count = lax.axis_size(axis)
    return lax.ppermute(x, axis, [(i, i ^ mask) for i in range(count)])


def body(energies, h_blocks, couplings, shift_real, shift_rate, screened, sources, counts):
    segs = lax.axis_size("seg")
    chips = lax.axis_size("energy") // cores
    first = lax.axis_index("energy") % cores == 0
    hams, links = h_blocks[0], couplings[0]
    one = jnp.where(first, hams[0], hams[2])
    two = jnp.where(first, hams[1], hams[3])
    lower = jnp.arange(64)[:, None] >= jnp.arange(64)[None, :]
    packed = jnp.concatenate(
        [jnp.where(lower, one[:, :64], one[:, 64:]), jnp.where(lower, two[:, :64], two[:, 64:])], 1
    )
    piece = jnp.concatenate(
        [
            jnp.where(first, links[0], links[2]),
            jnp.where(first, links[1], links[3]),
            packed,
            shift_real.reshape(2, 128),
            shift_rate.reshape(2, 128),
            jnp.broadcast_to(counts.astype(f32)[:, None], (4, 128)),
        ],
        0,
    )
    sent = [flipped_to(piece, "seg", k) for k in range(1, segs)]
    own = [settle(energies, piece)] + sent
    other = [flipped_to(x, "energy", 1) for x in [piece] + sent]
    greens = wire(own, other)
    near = [greens] + [flipped_to(greens, "energy", cores * k) for k in range(1, chips)]
    far = [flipped_to(x, "energy", 1) for x in near]
    return sum_shifts(sources, near, far, screened[:, 0])[None, None]


def solution(mesh):
    in_specs = (
        P("energy"),
        P("seg", None, None, None),
        P("seg", None, None, None),
        P("energy", "seg", None),
        P("energy", "seg", None),
        P(None, "seg", None, None, None),
        P("energy", None),
        P("seg"),
    )
    out_specs = P("energy", "seg", None, None, None)
    return jax.shard_map(body, mesh=mesh, in_specs=in_specs, out_specs=out_specs, check_vma=False)
```

```python
import jax
import jax.numpy as jnp
from jax import lax
from jax.experimental import pallas as pl
from jax.experimental.pallas import tpu as pltpu
from jax.sharding import PartitionSpec as P

broadening = 0.02
cores = 2
f32 = jnp.float32
bf16 = jnp.bfloat16
VMEM = pl.BlockSpec(memory_space=pltpu.VMEM)
SMEM = pl.BlockSpec(memory_space=pltpu.SMEM)


def column(slab, k, lane):
    return jnp.take_along_axis(slab, jnp.where(lane < 64, k, 64 + k), axis=1)


def row(slab, k):
    return jnp.broadcast_to(slab[k : k + 1, :], (8, 128))


def added(parts):
    while len(parts) > 1:
        parts = [a + b for a, b in zip(parts[::2], parts[1::2])]
    return parts[0]


def far_product(whole_r, whole_i, pr, pi, t):
    lane = lax.broadcasted_iota(jnp.int32, (8, 128), 1)
    keep = lane < 64
    source = (lane & 64) + 8 * t + (lane & 7)
    re = jnp.concatenate([jnp.take_along_axis(x, source, axis=1) for x in whole_r], 0)
    im = jnp.concatenate([jnp.take_along_axis(x, source, axis=1) for x in whole_i], 0)
    wide = lax.broadcasted_iota(jnp.int32, re.shape, 1)
    both = jnp.where((wide & 8) > 0, im, re)
    high = both.astype(bf16).astype(f32)
    left = jnp.where(((wide & 63) >> 4) == 1, both - high, high).astype(bf16)
    zero = jnp.zeros((8, 128), f32)
    empty = jnp.zeros((16, 256), bf16)
    right = []
    for kept in (keep, ~keep):
        r, i = jnp.where(kept, pr, zero), jnp.where(kept, pi, zero)
        high, low = split(
            jnp.concatenate([jnp.concatenate([r, i], 1), jnp.concatenate([-i, r], 1)], 0)
        )
        right += [high, high, low, empty]
    out = dot(left, jnp.concatenate(right, 0))
    return out[:, :128], out[:, 128:]


def panels(mr, mi):
    lane = lax.broadcasted_iota(jnp.int32, (8, 128), 1)
    sub = lax.broadcasted_iota(jnp.int32, (8, 128), 0)
    col = lane & 63
    for t in range(8):
        near = (t + 1) % 8
        far = [(t + d) % 8 for d in range(2, 8)]
        inside = (col >= 8 * t) & (col < 8 * t + 8)
        xr = [column(mr[t], 8 * t + j, lane) for j in range(8)]
        xi = [column(mi[t], 8 * t + j, lane) for j in range(8)]
        cr = [column(mr[near], 8 * t + j, lane) for j in range(8)]
        ci = [column(mi[near], 8 * t + j, lane) for j in range(8)]
        rr = jnp.where(inside, jnp.where(col == sub + 8 * t, 1.0, 0.0), mr[t])
        ri = jnp.where(inside, 0.0, mi[t])
        vr, vi = jnp.ones((8, 128), f32), jnp.zeros((8, 128), f32)
        for k in range(8):
            at = sub == k
            pr, pi = row(xr[k], k), row(xi[k], k)
            q = 1.0 / (pr * pr + pi * pi)
            er, ei = jnp.where(at, 0.0, xr[k]), jnp.where(at, 0.0, xi[k])
            fr, fi = er * pr + ei * pi, ei * pr - er * pi
            vr, vi = jnp.where(at, pr * q, vr), jnp.where(at, -(pi * q), vi)

            def step(yr, yi):
                ar, ai = row(yr, k), row(yi, k)
                wr, wi = fr * ar - fi * ai, fr * ai + fi * ar
                return yr - wr * q, yi - wi * q

            for j in range(k + 1, 8):
                xr[j], xi[j] = step(xr[j], xi[j])
            rr, ri = step(rr, ri)
        rr, ri = rr * vr - ri * vi, rr * vi + ri * vr
        lines = [(row(rr, j), row(ri, j)) for j in range(8)]
        more_r = added([cr[j] * lines[j][0] - ci[j] * lines[j][1] for j in range(8)])
        more_i = added([cr[j] * lines[j][1] + ci[j] * lines[j][0] for j in range(8)])
        mr[near] = jnp.where(inside, 0.0, mr[near]) - more_r
        mi[near] = jnp.where(inside, 0.0, mi[near]) - more_i
        out_r, out_i = far_product([mr[s] for s in far], [mi[s] for s in far], rr, ri, t)
        for n, s in enumerate(far):
            mr[s] = jnp.where(inside, 0.0, mr[s]) - out_r[8 * n : 8 * n + 8]
            mi[s] = jnp.where(inside, 0.0, mi[s]) - out_i[8 * n : 8 * n + 8]
        mr[t], mi[t] = rr, ri
        yield


def slabs(x):
    return [x[8 * s : 8 * s + 8] for s in range(8)]


def invert_pairs(pairs, beside=()):
    beside = iter(beside)
    held = [(slabs(zr), slabs(zi)) for zr, zi in pairs]
    for _ in zip(*[panels(mr, mi) for mr, mi in held]):
        work = next(beside, None)
        if work is not None:
            work()
    for work in beside:
        work()
    return [(jnp.concatenate(mr, 0), jnp.concatenate(mi, 0)) for mr, mi in held]


def low_lanes(x):
    return lax.broadcasted_iota(jnp.int32, x.shape, 1) < 64


def split(x):
    high = x.astype(bf16)
    return high, (x - high.astype(f32)).astype(bf16)


def diagonal(x):
    keep = low_lanes(x)
    zero = jnp.zeros_like(x)
    return jnp.concatenate([jnp.where(keep, x, zero), jnp.where(keep, zero, x)], 0)


def dot(a, b):
    return jnp.dot(a, b, preferred_element_type=f32)


def left_factor(qr, qi):
    rh, rl = split(qr)
    ih, il = split(qi)

    def whole(r, i):
        return jnp.concatenate(
            [jnp.concatenate([r, -i], 1), jnp.concatenate([i, r], 1)], 0
        )

    return jnp.concatenate([whole(rh, ih), whole(rl, il)], 0)


def right_factor(yr, yi):
    def whole(r, i):
        dr, di = diagonal(r), diagonal(i)
        return jnp.concatenate(
            [jnp.concatenate([dr, di], 1), jnp.concatenate([-di, dr], 1)], 0
        )

    rh, rl = split(yr)
    ih, il = split(yi)
    return whole(rh, ih), whole(rl, il)


def times_right(xr, xi, high, low):
    xh, xl = split(jnp.concatenate([xr, xi], 1))
    both = dot(jnp.concatenate([xh, xl], 0), high)
    out = both[:64] + (both[64:] + dot(xh, low))
    return out[:, :128], out[:, 128:]


def times_left(left, xr, xi):
    rh, rl = split(xr)
    ih, il = split(xi)
    right = jnp.concatenate(
        [
            jnp.concatenate([diagonal(rh), diagonal(rl)], 1),
            jnp.concatenate([diagonal(ih), diagonal(il)], 1),
        ],
        0,
    )
    out = dot(left, right)
    out = out[:128, :128] + (out[:128, 128:] + out[128:, :128])
    return out[:64], out[64:]


def swapped(x):
    return pltpu.roll(x, 64, 1)


def settle_kernel(energies_ref, in_ref, out_ref):
    out_ref[0:200] = in_ref[0:200]
    last = lax.broadcasted_iota(jnp.int32, (8, 128), 0) >= 6
    out_ref[200:208] = jnp.where(last, energies_ref[0], in_ref[200:208])


def settle(energies, piece):
    return pl.pallas_call(
        settle_kernel,
        out_shape=jax.ShapeDtypeStruct(piece.shape, f32),
        in_specs=[SMEM, VMEM],
        out_specs=VMEM,
        compiler_params=pltpu.CompilerParams(vmem_limit_bytes=4 * 2**20),
        name="settle",
    )(energies, piece)


def wire_kernel(segs, *refs):
    own = refs[:segs]
    other = refs[segs : 2 * segs]
    out_ref = refs[2 * segs]
    (u_ref, h_ref, d_ref, m_ref, at_ref, ar_ref, ai_ref, yright_ref, yleft_ref, g_ref, s_ref, k_ref, t_ref) = (
        refs[2 * segs + 1 :]
    )
    blocks = 2 * segs
    half = segs
    place, core = lax.axis_index("seg"), lax.axis_index("energy") & 1

    for k in range(segs):
        seg = jnp.bitwise_xor(place, k)
        for c, ref in ((core, own[k]), (1 - core, other[k])):
            u_ref[4 * seg + 2 * c] = ref[0:64]
            u_ref[4 * seg + 2 * c + 1] = ref[64:128]
            h_ref[2 * seg + c] = ref[128:192]
            d_ref[2 * seg + c] = ref[192:200]
        m_ref[seg] = own[k][200:208]
    energy = own[0][206:207]

    start = jnp.int32(0)
    first, used = jnp.int32(0), jnp.int32(0)
    for seg in range(segs):
        count = jnp.max(m_ref[seg, 4:5, :]).astype(jnp.int32)
        for k in range(4):
            at_ref[start + k] = 4 * seg + k
        first = jnp.where(seg == place, start, first)
        used = jnp.where(seg == place, count, used)
        start = start + count

    keep = low_lanes(jnp.zeros((64, 128), f32))
    rows = lax.broadcasted_iota(jnp.int32, (64, 128), 0)
    cols = lax.broadcasted_iota(jnp.int32, (64, 128), 1) & 63

    def prepare_block(i, carry):
        one, two = at_ref[i], at_ref[blocks - 1 - i]
        odd_one, odd_two = one & 1, two & 1
        raw_one, raw_two = h_ref[one >> 1], h_ref[two >> 1]
        flat_re = jnp.where(keep, raw_one, swapped(raw_two))
        flat_im = jnp.where(keep, swapped(raw_one), raw_two)
        turned = jnp.concatenate([raw_one, raw_two], 0).T
        odd = jnp.where(keep, odd_one, odd_two)
        held = ((rows >= cols).astype(jnp.int32) ^ odd) > 0
        line = jnp.where(keep[:8], d_ref[one >> 1], swapped(d_ref[two >> 1]))
        on = rows == cols
        real = jnp.where(held, flat_re, turned[:64])
        real = jnp.where(on & (odd > 0), jnp.concatenate([line] * 8, 0), real)
        imag = jnp.where(on, 0.0, jnp.where(held, flat_im, -turned[64:]))
        extra = []
        for base in (0, 2):
            line_one = m_ref[one >> 2, pl.ds(base + ((one >> 1) & 1), 1), :]
            line_two = m_ref[two >> 2, pl.ds(base + ((two >> 1) & 1), 1), :]
            line_one = pltpu.roll(jnp.broadcast_to(line_one, (8, 128)), 64 * odd_one, 1)
            line_two = pltpu.roll(jnp.broadcast_to(line_two, (8, 128)), 64 * (1 - odd_two), 1)
            line = jnp.where(keep[:8], line_one, line_two)
            extra.append(jnp.broadcast_to(line[:1], (64, 128)))
        ar_ref[i] = jnp.where(on, energy - extra[0], 0.0) - real
        ai_ref[i] = jnp.where(on, broadening + extra[1], 0.0) - imag
        return carry

    def prepare_link(i, carry):
        one, two = u_ref[at_ref[i]], u_ref[at_ref[blocks - i]]
        flat_re = jnp.where(keep, one, swapped(two))
        flat_im = jnp.where(keep, swapped(one), two)
        turned = jnp.concatenate([one, two], 0).T
        turned_re, turned_im = turned[:64], -turned[64:]
        y = jnp.where(keep, flat_re, turned_re), jnp.where(keep, flat_im, turned_im)
        y_adjoint = jnp.where(keep, turned_re, flat_re), jnp.where(keep, turned_im, flat_im)
        high, low = right_factor(*y)
        yright_ref[i - 1, 0] = high
        yright_ref[i - 1, 1] = low
        yleft_ref[i - 1] = left_factor(*y_adjoint)
        return y, y_adjoint

    def long_wire():
        lax.fori_loop(0, half, prepare_block, 0)
        lax.fori_loop(1, half + 1, lambda i, carry: prepare_link(i, carry) and carry, 0)

        s_ref[...] = jnp.zeros_like(s_ref)

        def inward(i, carry):
            fr = ar_ref[i] - s_ref[0]
            fi = ai_ref[i] - s_ref[1]
            ((gr, gi),) = invert_pairs([(fr, fi)])
            g_ref[i, 0] = gr
            g_ref[i, 1] = gi

            @pl.when(i < half)
            def _():
                tr, ti = times_right(gr, gi, yright_ref[i, 0], yright_ref[i, 1])
                t_ref[i] = left_factor(tr, ti)
                sr, si = times_left(yleft_ref[i], tr, ti)
                kr, ki = times_left(yleft_ref[i], gr, gi)
                high, low = right_factor(kr, ki)
                k_ref[i, 0] = high
                k_ref[i, 1] = low
                s_ref[0] = sr
                s_ref[1] = si

            @pl.when(i == half - 1)
            def _():
                s_ref[0] = swapped(s_ref[0])
                s_ref[1] = swapped(s_ref[1])
                ar_ref[half] = fr
                ai_ref[half] = fi

            return carry

        lax.fori_loop(0, half + 1, inward, 0)

        g_ref[half - 1] = g_ref[half]

        def outward(step, carry):
            i = half - 2 - step
            zr, zi = times_right(g_ref[i + 1, 0], g_ref[i + 1, 1], k_ref[i, 0], k_ref[i, 1])
            wr, wi = times_left(t_ref[i], zr, zi)
            g_ref[i, 0] = g_ref[i, 0] + wr
            g_ref[i, 1] = g_ref[i, 1] + wi
            return carry

        lax.fori_loop(0, half - 1, outward, 0)

    def wire_of_eight():
        v = {}

        def plus(x, y):
            return x[0] + y[0], x[1] + y[1]

        def minus(x, y):
            return x[0] - y[0], x[1] - y[1]

        def block(i):
            return ar_ref[i], ai_ref[i]

        def by_y(x, i):
            return times_right(*x, yright_ref[i - 1, 0], yright_ref[i - 1, 1])

        def adjoint_y_by(i, x):
            return times_left(yleft_ref[i - 1], *x)

        def do(step, *args):
            return lambda: step(*args)

        def link_two():
            y, y_adjoint = prepare_link(2, 0)
            v["y2_left"] = left_factor(*y)
            v["y2_adjoint_right"] = right_factor(*y_adjoint)

        def hold(name, product, *names):
            def run():
                v[name] = product(*[v[x] for x in names])

            return run

        def left_form(x):
            return left_factor(*x)

        def right_form(x):
            return right_factor(*x)

        def left_times(left, x):
            return times_left(left, *x)

        def times_right_form(x, right):
            return times_right(*x, *right)

        prepare_block(0, 0)
        prepare_block(2, 0)
        v["g0"], v["g2"] = invert_pairs(
            [block(0), block(2)],
            [
                do(prepare_link, 1, 0),
                link_two,
                do(prepare_block, 1, 0),
                do(prepare_link, 3, 0),
                do(prepare_block, 3, 0),
                do(prepare_link, 4, 0),
            ],
        )
        v["t0"] = by_y(v["g0"], 1)
        v["p_"] = left_times(v["y2_left"], v["g2"])
        first_one = minus(block(1), adjoint_y_by(1, v["t0"]))
        first_one = minus(first_one, times_right_form(v["p_"], v["y2_adjoint_right"]))

        def third():
            v["q_"] = adjoint_y_by(3, v["g2"])

        def fourth():
            v["f3"] = minus(block(3), by_y(v["q_"], 3))

        def w13():
            v["w13"] = right_form(by_y(v["p_"], 3))

        def w31():
            v["w31"] = left_form(times_right_form(v["q_"], v["y2_adjoint_right"]))

        def k0():
            v["k0"] = right_form(adjoint_y_by(1, v["g0"]))

        def q():
            v["q"] = by_y(v["g2"], 3)

        def p():
            v["p"] = left_form(times_right_form(v["g2"], v["y2_adjoint_right"]))

        def forms():
            v["t0_left"] = left_form(v["t0"])
            v["p_right"] = right_form(v["p_"])

        (v["g1"],) = invert_pairs([first_one], [third, w13, w31, fourth, k0, q, p, forms])
        v["m"] = times_right_form(v["g1"], v["w13"])
        f3 = minus(v["f3"], left_times(v["w31"], v["m"]))

        def base_zero():
            v["base0"] = plus(v["g0"], times_right_form(v["t0_g1"], v["k0"]))

        def base_two():
            v["base2"] = plus(v["g2"], times_right_form(v["p_g1"], v["p_right"]))

        def left_two():
            v["left2"] = left_form(plus(left_times(v["p"], v["m"]), v["q"]))

        def right_two():
            v["right2"] = right_form(plus(times_right_form(v["n"], v["p_right"]), v["q_"]))

        def left_zero():
            v["left0"] = left_form(left_times(v["t0_left"], v["m"]))

        def right_zero():
            v["right0"] = right_form(times_right_form(v["n"], v["k0"]))

        def ends():
            v["left1"] = left_form(v["m"])
            v["right1"] = right_form(v["n"])

        (g3,) = invert_pairs(
            [f3],
            [
                hold("n", left_times, "w31", "g1"),
                hold("t0_g1", left_times, "t0_left", "g1"),
                hold("p_g1", left_times, "p", "g1"),
                base_zero,
                base_two,
                left_two,
                right_two,
                ends,
            ],
        )
        across = adjoint_y_by(4, by_y(g3, 4))
        middle = minus(f3, (swapped(across[0]), swapped(across[1])))
        (g_middle,) = invert_pairs([middle], [left_zero, right_zero])
        g_ref[3, 0], g_ref[3, 1] = g_middle
        for i, base in ((0, "base0"), (1, "g1"), (2, "base2")):
            more = times_right_form(g_middle, v["right" + str(i)])
            g_ref[i, 0], g_ref[i, 1] = plus(v[base], left_times(v["left" + str(i)], more))

    if half == 4:
        wire_of_eight()
    else:
        long_wire()

    for k in range(4):
        block = jnp.minimum(first + k, blocks - 1)
        right = (block >= half).astype(jnp.int32)
        i = jnp.where(block >= half, blocks - 1 - block, block)
        re = pltpu.roll(g_ref[i, 0], 64 * right, 1)
        im = pltpu.roll(g_ref[i, 1], 64 * (1 - right), 1)
        live = (k < used).astype(f32)
        out_ref[k] = (jnp.where(keep, re, im) * live).astype(bf16)


def wire(own, other):
    segs = len(own)
    half = segs

    def kernel(*refs):
        wire_kernel(segs, *refs)

    return pl.pallas_call(
        kernel,
        out_shape=jax.ShapeDtypeStruct((4, 64, 128), bf16),
        in_specs=[VMEM] * (2 * segs),
        out_specs=VMEM,
        scratch_shapes=[
            pltpu.VMEM((4 * segs, 64, 128), f32),
            pltpu.VMEM((2 * segs, 64, 128), f32),
            pltpu.VMEM((2 * segs, 8, 128), f32),
            pltpu.VMEM((segs, 8, 128), f32),
            pltpu.SMEM((2 * segs + 4,), jnp.int32),
            pltpu.VMEM((half + 1, 64, 128), f32),
            pltpu.VMEM((half + 1, 64, 128), f32),
            pltpu.VMEM((half, 2, 256, 256), bf16),
            pltpu.VMEM((half, 256, 256), bf16),
            pltpu.VMEM((half + 1, 2, 64, 128), f32),
            pltpu.VMEM((2, 64, 128), f32),
            pltpu.VMEM((half, 2, 256, 256), bf16),
            pltpu.VMEM((half, 256, 256), bf16),
        ],
        compiler_params=pltpu.CompilerParams(vmem_limit_bytes=(8 + 2 * segs) * 2**20),
        name="wire",
    )(*own, *other)


def order_kernel(chips, sources_ref, screened_ref, *out_refs):
    energy = lax.axis_index("energy")
    for side, (plain_ref, other_ref) in enumerate((out_refs[:2], out_refs[2:])):
        for k in range(chips):
            wanted = ((energy >> 1) ^ k) * cores + ((energy & 1) ^ side)
            place, found = jnp.int32(0), jnp.int32(0)
            for j in range(screened_ref.shape[0]):
                hit = (sources_ref[0, j] == wanted).astype(jnp.int32)
                place, found = place + j * hit, found + hit
            for slot in range(4):
                weight = screened_ref[place, slot] * found.astype(f32)
                plain_ref[k, slot] = weight
                other_ref[k, slot] = swapped(weight)


def order_weights(chips, sources, screened):
    shape = jax.ShapeDtypeStruct((chips,) + screened.shape[1:], f32)

    def kernel(*refs):
        order_kernel(chips, *refs)

    return pl.pallas_call(
        kernel,
        out_shape=[shape] * 4,
        in_specs=[SMEM, VMEM],
        out_specs=[VMEM] * 4,
        compiler_params=pltpu.CompilerParams(vmem_limit_bytes=(4 + chips) * 2**20),
        name="order_weights",
    )(sources, screened)


def sum_kernel(pieces, plain_ref, other_ref, *refs):
    greens, rest = refs[:pieces], refs[pieces:]
    keep = low_lanes(jnp.zeros((64, 128), f32))

    def total(slot):
        direct = jnp.zeros((64, 128), f32)
        crossed = jnp.zeros((64, 128), f32)
        for k in range(pieces):
            green = greens[k][slot].astype(f32)
            direct = direct + green * plain_ref[k, slot]
            crossed = crossed + green * other_ref[k, slot]
        return jnp.where(keep, direct - swapped(direct), crossed + swapped(crossed))

    if len(rest) == 1:
        for slot in range(4):
            rest[0][slot] = total(slot)
    else:
        before_ref, out_ref, done_ref, sem = rest
        copies = []
        for slot in range(4):
            done_ref[slot] = total(slot) + before_ref[slot]
            copies.append(pltpu.make_async_copy(done_ref.at[slot], out_ref.at[slot], sem.at[slot]))
            copies[-1].start()
        for copy in copies:
            copy.wait()


def sum_near(greens, plain, other):
    def kernel(*refs):
        sum_kernel(len(greens), *refs)

    return pl.pallas_call(
        kernel,
        out_shape=jax.ShapeDtypeStruct(plain.shape[1:], f32),
        in_specs=[VMEM] * (2 + len(greens)),
        out_specs=VMEM,
        compiler_params=pltpu.CompilerParams(vmem_limit_bytes=(4 + len(greens)) * 2**20),
        name="sum_near",
    )(plain, other, *greens)


def sum_far(greens, plain, other, before):
    def kernel(*refs):
        sum_kernel(len(greens), *refs)

    return pl.pallas_call(
        kernel,
        out_shape=jax.ShapeDtypeStruct(plain.shape[1:], f32),
        in_specs=[VMEM] * (3 + len(greens)),
        out_specs=pl.BlockSpec(memory_space=pl.ANY),
        scratch_shapes=[pltpu.VMEM(plain.shape[1:], f32), pltpu.SemaphoreType.DMA((4,))],
        compiler_params=pltpu.CompilerParams(vmem_limit_bytes=(4 + len(greens)) * 2**20),
        name="sum_far",
    )(plain, other, *greens, before)


def flipped_to(x, axis, mask):
    count = lax.axis_size(axis)
    return lax.ppermute(x, axis, [(i, i ^ mask) for i in range(count)])


def body(energies, h_blocks, couplings, shift_real, shift_rate, screened, sources, counts):
    segs = lax.axis_size("seg")
    chips = lax.axis_size("energy") // cores
    first = lax.axis_index("energy") % cores == 0
    hams, links = h_blocks[0], couplings[0]
    one = jnp.where(first, hams[0], hams[2])
    two = jnp.where(first, hams[1], hams[3])
    lower = jnp.arange(64)[:, None] >= jnp.arange(128)[None, :] % 64
    group = jnp.arange(128)[None, :] % 64 // 8
    line = sum(jnp.where(group == n, two[8 * n : 8 * n + 8], 0.0) for n in range(8))

    def at_rows(x, start):
        return jnp.pad(x, ((start, 208 - start - x.shape[0]), (0, 0)))

    piece = (
        at_rows(jnp.where(first, links[0], links[2]), 0)
        + at_rows(jnp.where(first, links[1], links[3]), 64)
        + at_rows(jnp.where(lower, one, two), 128)
        + at_rows(line, 192)
        + at_rows(shift_real.reshape(2, 128), 200)
        + at_rows(shift_rate.reshape(2, 128), 202)
        + at_rows(jnp.broadcast_to(counts.astype(f32)[:, None], (4, 128)), 204)
    )
    sent = [flipped_to(piece, "seg", k) for k in range(1, segs)]
    own = [settle(energies, piece)] + sent
    other = [flipped_to(x, "energy", 1) for x in [piece] + sent]
    greens = wire(own, other)
    near = [greens] + [flipped_to(greens, "energy", cores * k) for k in range(1, chips)]
    far = [flipped_to(x, "energy", 1) for x in near]
    plain_near, other_near, plain_far, other_far = order_weights(chips, sources, screened[:, 0])
    partial = sum_near(near, plain_near, other_near)
    return sum_far(far, plain_far, other_far, partial)[None, None]


def solution(mesh):
    in_specs = (
        P("energy"),
        P("seg", None, None, None),
        P("seg", None, None, None),
        P("energy", "seg", None),
        P("energy", "seg", None),
        P(None, "seg", None, None, None),
        P("energy", None),
        P("seg"),
    )
    out_specs = P("energy", "seg", None, None, None)
    return jax.shard_map(body, mesh=mesh, in_specs=in_specs, out_specs=out_specs, check_vma=False)
```

```python
import jax
import jax.numpy as jnp
from jax import lax
from jax.experimental import pallas as pl
from jax.experimental.pallas import tpu as pltpu
from jax.sharding import PartitionSpec as P

broadening = 0.02
cores = 2
f32 = jnp.float32
bf16 = jnp.bfloat16
VMEM = pl.BlockSpec(memory_space=pltpu.VMEM)
SMEM = pl.BlockSpec(memory_space=pltpu.SMEM)


def column(slab, k, lane):
    return jnp.take_along_axis(slab, jnp.where(lane < 64, k, 64 + k), axis=1)


def row(slab, k):
    return jnp.broadcast_to(slab[k : k + 1, :], (8, 128))


def added(parts):
    while len(parts) > 1:
        parts = [a + b for a, b in zip(parts[::2], parts[1::2])]
    return parts[0]


def far_product(whole_r, whole_i, pr, pi, t):
    lane = lax.broadcasted_iota(jnp.int32, (8, 128), 1)
    keep = lane < 64
    source = (lane & 64) + 8 * t + (lane & 7)
    re = jnp.concatenate([jnp.take_along_axis(x, source, axis=1) for x in whole_r], 0)
    im = jnp.concatenate([jnp.take_along_axis(x, source, axis=1) for x in whole_i], 0)
    wide = lax.broadcasted_iota(jnp.int32, re.shape, 1)
    both = jnp.where((wide & 8) > 0, im, re)
    high = both.astype(bf16).astype(f32)
    left = jnp.where(((wide & 63) >> 4) == 1, both - high, high).astype(bf16)
    zero = jnp.zeros((8, 128), f32)
    empty = jnp.zeros((16, 256), bf16)
    right = []
    for kept in (keep, ~keep):
        r, i = jnp.where(kept, pr, zero), jnp.where(kept, pi, zero)
        high, low = split(
            jnp.concatenate([jnp.concatenate([r, i], 1), jnp.concatenate([-i, r], 1)], 0)
        )
        right += [high, high, low, empty]
    out = dot(left, jnp.concatenate(right, 0))
    return out[:, :128], out[:, 128:]


def panels(mr, mi):
    lane = lax.broadcasted_iota(jnp.int32, (8, 128), 1)
    sub = lax.broadcasted_iota(jnp.int32, (8, 128), 0)
    col = lane & 63
    for t in range(8):
        near = (t + 1) % 8
        far = [(t + d) % 8 for d in range(2, 8)]
        inside = (col >= 8 * t) & (col < 8 * t + 8)
        xr = [column(mr[t], 8 * t + j, lane) for j in range(8)]
        xi = [column(mi[t], 8 * t + j, lane) for j in range(8)]
        cr = [column(mr[near], 8 * t + j, lane) for j in range(8)]
        ci = [column(mi[near], 8 * t + j, lane) for j in range(8)]
        rr = jnp.where(inside, jnp.where(col == sub + 8 * t, 1.0, 0.0), mr[t])
        ri = jnp.where(inside, 0.0, mi[t])
        vr, vi = jnp.ones((8, 128), f32), jnp.zeros((8, 128), f32)
        for k in range(8):
            at = sub == k
            pr, pi = row(xr[k], k), row(xi[k], k)
            q = 1.0 / (pr * pr + pi * pi)
            er, ei = jnp.where(at, 0.0, xr[k]), jnp.where(at, 0.0, xi[k])
            fr, fi = er * pr + ei * pi, ei * pr - er * pi
            vr, vi = jnp.where(at, pr * q, vr), jnp.where(at, -(pi * q), vi)

            def step(yr, yi):
                ar, ai = row(yr, k), row(yi, k)
                wr, wi = fr * ar - fi * ai, fr * ai + fi * ar
                return yr - wr * q, yi - wi * q

            for j in range(k + 1, 8):
                xr[j], xi[j] = step(xr[j], xi[j])
            rr, ri = step(rr, ri)
        rr, ri = rr * vr - ri * vi, rr * vi + ri * vr
        lines = [(row(rr, j), row(ri, j)) for j in range(8)]
        more_r = added([cr[j] * lines[j][0] - ci[j] * lines[j][1] for j in range(8)])
        more_i = added([cr[j] * lines[j][1] + ci[j] * lines[j][0] for j in range(8)])
        mr[near] = jnp.where(inside, 0.0, mr[near]) - more_r
        mi[near] = jnp.where(inside, 0.0, mi[near]) - more_i
        out_r, out_i = far_product([mr[s] for s in far], [mi[s] for s in far], rr, ri, t)
        for n, s in enumerate(far):
            mr[s] = jnp.where(inside, 0.0, mr[s]) - out_r[8 * n : 8 * n + 8]
            mi[s] = jnp.where(inside, 0.0, mi[s]) - out_i[8 * n : 8 * n + 8]
        mr[t], mi[t] = rr, ri
        yield


def slabs(x):
    return [x[8 * s : 8 * s + 8] for s in range(8)]


def invert_pairs(pairs, beside=()):
    beside = iter(beside)
    held = [(slabs(zr), slabs(zi)) for zr, zi in pairs]
    for _ in zip(*[panels(mr, mi) for mr, mi in held]):
        work = next(beside, None)
        if work is not None:
            work()
    for work in beside:
        work()
    return [(jnp.concatenate(mr, 0), jnp.concatenate(mi, 0)) for mr, mi in held]


def low_lanes(x):
    return lax.broadcasted_iota(jnp.int32, x.shape, 1) < 64


def split(x):
    high = x.astype(bf16)
    return high, (x - high.astype(f32)).astype(bf16)


def diagonal(x):
    keep = low_lanes(x)
    zero = jnp.zeros_like(x)
    return jnp.concatenate([jnp.where(keep, x, zero), jnp.where(keep, zero, x)], 0)


def dot(a, b):
    return jnp.dot(a, b, preferred_element_type=f32)


def left_factor(qr, qi):
    rh, rl = split(qr)
    ih, il = split(qi)

    def whole(r, i):
        return jnp.concatenate(
            [jnp.concatenate([r, -i], 1), jnp.concatenate([i, r], 1)], 0
        )

    return jnp.concatenate([whole(rh, ih), whole(rl, il)], 0)


def right_factor(yr, yi):
    def whole(r, i):
        dr, di = diagonal(r), diagonal(i)
        return jnp.concatenate(
            [jnp.concatenate([dr, di], 1), jnp.concatenate([-di, dr], 1)], 0
        )

    rh, rl = split(yr)
    ih, il = split(yi)
    return whole(rh, ih), whole(rl, il)


def times_right(xr, xi, high, low):
    xh, xl = split(jnp.concatenate([xr, xi], 1))
    both = dot(jnp.concatenate([xh, xl], 0), high)
    out = both[:64] + (both[64:] + dot(xh, low))
    return out[:, :128], out[:, 128:]


def times_left(left, xr, xi):
    rh, rl = split(xr)
    ih, il = split(xi)
    right = jnp.concatenate(
        [
            jnp.concatenate([diagonal(rh), diagonal(rl)], 1),
            jnp.concatenate([diagonal(ih), diagonal(il)], 1),
        ],
        0,
    )
    out = dot(left, right)
    out = out[:128, :128] + (out[:128, 128:] + out[128:, :128])
    return out[:64], out[64:]


def swapped(x):
    return pltpu.roll(x, 64, 1)


def settle_kernel(energies_ref, in_ref, out_ref):
    out_ref[0:200] = in_ref[0:200]
    last = lax.broadcasted_iota(jnp.int32, (8, 128), 0) >= 6
    out_ref[200:208] = jnp.where(last, energies_ref[0], in_ref[200:208])


def settle(energies, piece):
    return pl.pallas_call(
        settle_kernel,
        out_shape=jax.ShapeDtypeStruct(piece.shape, f32),
        in_specs=[SMEM, VMEM],
        out_specs=VMEM,
        compiler_params=pltpu.CompilerParams(vmem_limit_bytes=4 * 2**20),
        name="settle",
    )(energies, piece)


def wire_kernel(segs, *refs):
    other = refs[:segs][::-1]
    own = refs[segs : 2 * segs][::-1]
    out_ref = refs[2 * segs]
    (u_ref, h_ref, d_ref, m_ref, at_ref, ar_ref, ai_ref, yright_ref, yleft_ref, g_ref, s_ref, k_ref, t_ref) = (
        refs[2 * segs + 1 :]
    )
    blocks = 2 * segs
    half = segs
    place, core = lax.axis_index("seg"), lax.axis_index("energy") & 1

    for k in range(segs):
        seg = jnp.bitwise_xor(place, k)
        for c, ref in ((core, own[k]), (1 - core, other[k])):
            u_ref[4 * seg + 2 * c] = ref[0:64]
            u_ref[4 * seg + 2 * c + 1] = ref[64:128]
            h_ref[2 * seg + c] = ref[128:192]
            d_ref[2 * seg + c] = ref[192:200]
        m_ref[seg] = own[k][200:208]
    energy = own[0][206:207]

    start = jnp.int32(0)
    first, used = jnp.int32(0), jnp.int32(0)
    for seg in range(segs):
        count = jnp.max(m_ref[seg, 4:5, :]).astype(jnp.int32)
        for k in range(4):
            at_ref[start + k] = 4 * seg + k
        first = jnp.where(seg == place, start, first)
        used = jnp.where(seg == place, count, used)
        start = start + count

    keep = low_lanes(jnp.zeros((64, 128), f32))
    rows = lax.broadcasted_iota(jnp.int32, (64, 128), 0)
    cols = lax.broadcasted_iota(jnp.int32, (64, 128), 1) & 63

    def prepare_block(i, carry):
        one, two = at_ref[i], at_ref[blocks - 1 - i]
        odd_one, odd_two = one & 1, two & 1
        raw_one, raw_two = h_ref[one >> 1], h_ref[two >> 1]
        flat_re = jnp.where(keep, raw_one, swapped(raw_two))
        flat_im = jnp.where(keep, swapped(raw_one), raw_two)
        turned = jnp.concatenate([raw_one, raw_two], 0).T
        odd = jnp.where(keep, odd_one, odd_two)
        held = ((rows >= cols).astype(jnp.int32) ^ odd) > 0
        line = jnp.where(keep[:8], d_ref[one >> 1], swapped(d_ref[two >> 1]))
        on = rows == cols
        real = jnp.where(held, flat_re, turned[:64])
        real = jnp.where(on & (odd > 0), jnp.concatenate([line] * 8, 0), real)
        imag = jnp.where(on, 0.0, jnp.where(held, flat_im, -turned[64:]))
        extra = []
        for base in (0, 2):
            line_one = m_ref[one >> 2, pl.ds(base + ((one >> 1) & 1), 1), :]
            line_two = m_ref[two >> 2, pl.ds(base + ((two >> 1) & 1), 1), :]
            line_one = pltpu.roll(jnp.broadcast_to(line_one, (8, 128)), 64 * odd_one, 1)
            line_two = pltpu.roll(jnp.broadcast_to(line_two, (8, 128)), 64 * (1 - odd_two), 1)
            line = jnp.where(keep[:8], line_one, line_two)
            extra.append(jnp.broadcast_to(line[:1], (64, 128)))
        ar_ref[i] = jnp.where(on, energy - extra[0], 0.0) - real
        ai_ref[i] = jnp.where(on, broadening + extra[1], 0.0) - imag
        return carry

    def prepare_link(i, carry):
        one, two = u_ref[at_ref[i]], u_ref[at_ref[blocks - i]]
        flat_re = jnp.where(keep, one, swapped(two))
        flat_im = jnp.where(keep, swapped(one), two)
        turned = jnp.concatenate([one, two], 0).T
        turned_re, turned_im = turned[:64], -turned[64:]
        y = jnp.where(keep, flat_re, turned_re), jnp.where(keep, flat_im, turned_im)
        y_adjoint = jnp.where(keep, turned_re, flat_re), jnp.where(keep, turned_im, flat_im)
        high, low = right_factor(*y)
        yright_ref[i - 1, 0] = high
        yright_ref[i - 1, 1] = low
        yleft_ref[i - 1] = left_factor(*y_adjoint)
        return y, y_adjoint

    def long_wire():
        lax.fori_loop(0, half, prepare_block, 0)
        lax.fori_loop(1, half + 1, lambda i, carry: prepare_link(i, carry) and carry, 0)

        s_ref[...] = jnp.zeros_like(s_ref)

        def inward(i, carry):
            fr = ar_ref[i] - s_ref[0]
            fi = ai_ref[i] - s_ref[1]
            ((gr, gi),) = invert_pairs([(fr, fi)])
            g_ref[i, 0] = gr
            g_ref[i, 1] = gi

            @pl.when(i < half)
            def _():
                tr, ti = times_right(gr, gi, yright_ref[i, 0], yright_ref[i, 1])
                t_ref[i] = left_factor(tr, ti)
                sr, si = times_left(yleft_ref[i], tr, ti)
                kr, ki = times_left(yleft_ref[i], gr, gi)
                high, low = right_factor(kr, ki)
                k_ref[i, 0] = high
                k_ref[i, 1] = low
                s_ref[0] = sr
                s_ref[1] = si

            @pl.when(i == half - 1)
            def _():
                s_ref[0] = swapped(s_ref[0])
                s_ref[1] = swapped(s_ref[1])
                ar_ref[half] = fr
                ai_ref[half] = fi

            return carry

        lax.fori_loop(0, half + 1, inward, 0)

        g_ref[half - 1] = g_ref[half]

        def outward(step, carry):
            i = half - 2 - step
            zr, zi = times_right(g_ref[i + 1, 0], g_ref[i + 1, 1], k_ref[i, 0], k_ref[i, 1])
            wr, wi = times_left(t_ref[i], zr, zi)
            g_ref[i, 0] = g_ref[i, 0] + wr
            g_ref[i, 1] = g_ref[i, 1] + wi
            return carry

        lax.fori_loop(0, half - 1, outward, 0)

    def wire_of_eight():
        v = {}

        def plus(x, y):
            return x[0] + y[0], x[1] + y[1]

        def minus(x, y):
            return x[0] - y[0], x[1] - y[1]

        def block(i):
            return ar_ref[i], ai_ref[i]

        def by_y(x, i):
            return times_right(*x, yright_ref[i - 1, 0], yright_ref[i - 1, 1])

        def adjoint_y_by(i, x):
            return times_left(yleft_ref[i - 1], *x)

        def do(step, *args):
            return lambda: step(*args)

        def link_two():
            y, y_adjoint = prepare_link(2, 0)
            v["y2_left"] = left_factor(*y)
            v["y2_adjoint_right"] = right_factor(*y_adjoint)

        def hold(name, product, *names):
            def run():
                v[name] = product(*[v[x] for x in names])

            return run

        def left_form(x):
            return left_factor(*x)

        def right_form(x):
            return right_factor(*x)

        def left_times(left, x):
            return times_left(left, *x)

        def times_right_form(x, right):
            return times_right(*x, *right)

        prepare_block(0, 0)
        prepare_block(2, 0)
        v["g0"], v["g2"] = invert_pairs(
            [block(0), block(2)],
            [
                do(prepare_link, 1, 0),
                link_two,
                do(prepare_block, 1, 0),
                do(prepare_link, 3, 0),
                do(prepare_block, 3, 0),
                do(prepare_link, 4, 0),
            ],
        )
        v["t0"] = by_y(v["g0"], 1)
        v["p_"] = left_times(v["y2_left"], v["g2"])
        first_one = minus(block(1), adjoint_y_by(1, v["t0"]))
        first_one = minus(first_one, times_right_form(v["p_"], v["y2_adjoint_right"]))

        def third():
            v["q_"] = adjoint_y_by(3, v["g2"])

        def fourth():
            v["f3"] = minus(block(3), by_y(v["q_"], 3))

        def w13():
            v["w13"] = right_form(by_y(v["p_"], 3))

        def w31():
            v["w31"] = left_form(times_right_form(v["q_"], v["y2_adjoint_right"]))

        def k0():
            v["k0"] = right_form(adjoint_y_by(1, v["g0"]))

        def q():
            v["q"] = by_y(v["g2"], 3)

        def p():
            v["p"] = left_form(times_right_form(v["g2"], v["y2_adjoint_right"]))

        def forms():
            v["t0_left"] = left_form(v["t0"])
            v["p_right"] = right_form(v["p_"])

        (v["g1"],) = invert_pairs([first_one], [third, w13, w31, fourth, k0, q, p, forms])
        v["m"] = times_right_form(v["g1"], v["w13"])
        f3 = minus(v["f3"], left_times(v["w31"], v["m"]))

        def base_zero():
            v["base0"] = plus(v["g0"], times_right_form(v["t0_g1"], v["k0"]))

        def base_two():
            v["base2"] = plus(v["g2"], times_right_form(v["p_g1"], v["p_right"]))

        def left_two():
            v["left2"] = left_form(plus(left_times(v["p"], v["m"]), v["q"]))

        def right_two():
            v["right2"] = right_form(plus(times_right_form(v["n"], v["p_right"]), v["q_"]))

        def left_zero():
            v["left0"] = left_form(left_times(v["t0_left"], v["m"]))

        def right_zero():
            v["right0"] = right_form(times_right_form(v["n"], v["k0"]))

        def ends():
            v["left1"] = left_form(v["m"])
            v["right1"] = right_form(v["n"])

        (g3,) = invert_pairs(
            [f3],
            [
                hold("n", left_times, "w31", "g1"),
                hold("t0_g1", left_times, "t0_left", "g1"),
                hold("p_g1", left_times, "p", "g1"),
                base_zero,
                base_two,
                left_two,
                right_two,
                ends,
            ],
        )
        across = adjoint_y_by(4, by_y(g3, 4))
        middle = minus(f3, (swapped(across[0]), swapped(across[1])))
        (g_middle,) = invert_pairs([middle], [left_zero, right_zero])
        g_ref[3, 0], g_ref[3, 1] = g_middle
        for i, base in ((0, "base0"), (1, "g1"), (2, "base2")):
            more = times_right_form(g_middle, v["right" + str(i)])
            g_ref[i, 0], g_ref[i, 1] = plus(v[base], left_times(v["left" + str(i)], more))

    if half == 4:
        wire_of_eight()
    else:
        long_wire()

    for k in range(4):
        block = jnp.minimum(first + k, blocks - 1)
        right = (block >= half).astype(jnp.int32)
        i = jnp.where(block >= half, blocks - 1 - block, block)
        re = pltpu.roll(g_ref[i, 0], 64 * right, 1)
        im = pltpu.roll(g_ref[i, 1], 64 * (1 - right), 1)
        live = (k < used).astype(f32)
        out_ref[k] = (jnp.where(keep, re, im) * live).astype(bf16)


def wire(own, other):
    segs = len(own)
    half = segs

    def kernel(*refs):
        wire_kernel(segs, *refs)

    return pl.pallas_call(
        kernel,
        out_shape=jax.ShapeDtypeStruct((4, 64, 128), bf16),
        in_specs=[VMEM] * (2 * segs),
        out_specs=VMEM,
        scratch_shapes=[
            pltpu.VMEM((4 * segs, 64, 128), f32),
            pltpu.VMEM((2 * segs, 64, 128), f32),
            pltpu.VMEM((2 * segs, 8, 128), f32),
            pltpu.VMEM((segs, 8, 128), f32),
            pltpu.SMEM((2 * segs + 4,), jnp.int32),
            pltpu.VMEM((half + 1, 64, 128), f32),
            pltpu.VMEM((half + 1, 64, 128), f32),
            pltpu.VMEM((half, 2, 256, 256), bf16),
            pltpu.VMEM((half, 256, 256), bf16),
            pltpu.VMEM((half + 1, 2, 64, 128), f32),
            pltpu.VMEM((2, 64, 128), f32),
            pltpu.VMEM((half, 2, 256, 256), bf16),
            pltpu.VMEM((half, 256, 256), bf16),
        ],
        compiler_params=pltpu.CompilerParams(vmem_limit_bytes=(8 + 2 * segs) * 2**20),
        name="wire",
    )(*other[::-1], *own[::-1])


def order_kernel(chips, sources_ref, screened_ref, *out_refs):
    energy = lax.axis_index("energy")
    for side, (plain_ref, other_ref) in enumerate((out_refs[:2], out_refs[2:])):
        for k in range(chips):
            wanted = ((energy >> 1) ^ k) * cores + ((energy & 1) ^ side)
            place, found = jnp.int32(0), jnp.int32(0)
            for j in range(screened_ref.shape[0]):
                hit = (sources_ref[0, j] == wanted).astype(jnp.int32)
                place, found = place + j * hit, found + hit
            for slot in range(4):
                weight = screened_ref[place, slot] * found.astype(f32)
                plain_ref[k, slot] = weight
                other_ref[k, slot] = swapped(weight)


def order_weights(chips, sources, screened):
    shape = jax.ShapeDtypeStruct((chips,) + screened.shape[1:], f32)

    def kernel(*refs):
        order_kernel(chips, *refs)

    return pl.pallas_call(
        kernel,
        out_shape=[shape] * 4,
        in_specs=[SMEM, VMEM],
        out_specs=[VMEM] * 4,
        compiler_params=pltpu.CompilerParams(vmem_limit_bytes=(4 + chips) * 2**20),
        name="order_weights",
    )(sources, screened)


def sum_kernel(pieces, plain_ref, other_ref, *refs):
    greens, rest = refs[:pieces], refs[pieces:]
    keep = low_lanes(jnp.zeros((64, 128), f32))

    def total(slot):
        direct = jnp.zeros((64, 128), f32)
        crossed = jnp.zeros((64, 128), f32)
        for k in range(pieces):
            green = greens[k][slot].astype(f32)
            direct = direct + green * plain_ref[k, slot]
            crossed = crossed + green * other_ref[k, slot]
        return jnp.where(keep, direct - swapped(direct), crossed + swapped(crossed))

    if len(rest) == 1:
        for slot in range(4):
            rest[0][slot] = total(slot)
    else:
        before_ref, out_ref, done_ref, sem = rest
        copies = []
        for slot in range(4):
            done_ref[slot] = total(slot) + before_ref[slot]
            copies.append(pltpu.make_async_copy(done_ref.at[slot], out_ref.at[slot], sem.at[slot]))
            copies[-1].start()
        for copy in copies:
            copy.wait()


def sum_near(greens, plain, other):
    def kernel(*refs):
        sum_kernel(len(greens), *refs)

    return pl.pallas_call(
        kernel,
        out_shape=jax.ShapeDtypeStruct(plain.shape[1:], f32),
        in_specs=[VMEM] * (2 + len(greens)),
        out_specs=VMEM,
        compiler_params=pltpu.CompilerParams(vmem_limit_bytes=(4 + len(greens)) * 2**20),
        name="sum_near",
    )(plain, other, *greens)


def sum_far(greens, plain, other, before):
    def kernel(*refs):
        sum_kernel(len(greens), *refs)

    return pl.pallas_call(
        kernel,
        out_shape=jax.ShapeDtypeStruct(plain.shape[1:], f32),
        in_specs=[VMEM] * (3 + len(greens)),
        out_specs=pl.BlockSpec(memory_space=pl.ANY),
        scratch_shapes=[pltpu.VMEM(plain.shape[1:], f32), pltpu.SemaphoreType.DMA((4,))],
        compiler_params=pltpu.CompilerParams(vmem_limit_bytes=(4 + len(greens)) * 2**20),
        name="sum_far",
    )(plain, other, *greens, before)


def flipped_to(x, axis, mask):
    count = lax.axis_size(axis)
    return lax.ppermute(x, axis, [(i, i ^ mask) for i in range(count)])


def body(energies, h_blocks, couplings, shift_real, shift_rate, screened, sources, counts):
    segs = lax.axis_size("seg")
    chips = lax.axis_size("energy") // cores
    first = lax.axis_index("energy") % cores == 0
    hams, links = h_blocks[0], couplings[0]
    one = jnp.where(first, hams[0], hams[2])
    two = jnp.where(first, hams[1], hams[3])
    lower = jnp.arange(64)[:, None] >= jnp.arange(128)[None, :] % 64
    group = jnp.arange(128)[None, :] % 64 // 8
    line = sum(jnp.where(group == n, two[8 * n : 8 * n + 8], 0.0) for n in range(8))

    def at_rows(x, start):
        return jnp.pad(x, ((start, 208 - start - x.shape[0]), (0, 0)))

    piece = (
        at_rows(jnp.where(first, links[0], links[2]), 0)
        + at_rows(jnp.where(first, links[1], links[3]), 64)
        + at_rows(jnp.where(lower, one, two), 128)
        + at_rows(line, 192)
        + at_rows(shift_real.reshape(2, 128), 200)
        + at_rows(shift_rate.reshape(2, 128), 202)
        + at_rows(jnp.broadcast_to(counts.astype(f32)[:, None], (4, 128)), 204)
    )
    sent = [flipped_to(piece, "seg", k) for k in range(1, segs)]
    own = [settle(energies, piece)] + sent
    other = [flipped_to(x, "energy", 1) for x in [piece] + sent]
    greens = wire(own, other)
    near = [greens] + [flipped_to(greens, "energy", cores * k) for k in range(1, chips)]
    far = [flipped_to(x, "energy", 1) for x in near]
    plain_near, other_near, plain_far, other_far = order_weights(chips, sources, screened[:, 0])
    partial = sum_near(near, plain_near, other_near)
    return sum_far(far, plain_far, other_far, partial)[None, None]


def solution(mesh):
    in_specs = (
        P("energy"),
        P("seg", None, None, None),
        P("seg", None, None, None),
        P("energy", "seg", None),
        P("energy", "seg", None),
        P(None, "seg", None, None, None),
        P("energy", None),
        P("seg"),
    )
    out_specs = P("energy", "seg", None, None, None)
    return jax.shard_map(body, mesh=mesh, in_specs=in_specs, out_specs=out_specs, check_vma=False)
```

```python
import jax
import jax.numpy as jnp
from jax import lax
from jax.experimental import pallas as pl
from jax.experimental.pallas import tpu as pltpu
from jax.sharding import PartitionSpec as P

broadening = 0.02
cores = 2
f32 = jnp.float32
bf16 = jnp.bfloat16
VMEM = pl.BlockSpec(memory_space=pltpu.VMEM)
SMEM = pl.BlockSpec(memory_space=pltpu.SMEM)


def column(slab, k, lane):
    return jnp.take_along_axis(slab, jnp.where(lane < 64, k, 64 + k), axis=1)


def row(slab, k):
    return jnp.broadcast_to(slab[k : k + 1, :], (8, 128))


def added(parts):
    while len(parts) > 1:
        parts = [a + b for a, b in zip(parts[::2], parts[1::2])]
    return parts[0]


def far_product(whole_r, whole_i, pr, pi, t):
    lane = lax.broadcasted_iota(jnp.int32, (8, 128), 1)
    keep = lane < 64
    source = (lane & 64) + 8 * t + (lane & 7)
    re = jnp.concatenate([jnp.take_along_axis(x, source, axis=1) for x in whole_r], 0)
    im = jnp.concatenate([jnp.take_along_axis(x, source, axis=1) for x in whole_i], 0)
    wide = lax.broadcasted_iota(jnp.int32, re.shape, 1)
    both = jnp.where((wide & 8) > 0, im, re)
    high = both.astype(bf16).astype(f32)
    left = jnp.where(((wide & 63) >> 4) == 1, both - high, high).astype(bf16)
    zero = jnp.zeros((8, 128), f32)
    empty = jnp.zeros((16, 256), bf16)
    right = []
    for kept in (keep, ~keep):
        r, i = jnp.where(kept, pr, zero), jnp.where(kept, pi, zero)
        high, low = split(
            jnp.concatenate([jnp.concatenate([r, i], 1), jnp.concatenate([-i, r], 1)], 0)
        )
        right += [high, high, low, empty]
    out = dot(left, jnp.concatenate(right, 0))
    return out[:, :128], out[:, 128:]


def panels(mr, mi):
    lane = lax.broadcasted_iota(jnp.int32, (8, 128), 1)
    sub = lax.broadcasted_iota(jnp.int32, (8, 128), 0)
    col = lane & 63
    for t in range(8):
        near = (t + 1) % 8
        far = [(t + d) % 8 for d in range(2, 8)]
        inside = (col >= 8 * t) & (col < 8 * t + 8)
        xr = [column(mr[t], 8 * t + j, lane) for j in range(8)]
        xi = [column(mi[t], 8 * t + j, lane) for j in range(8)]
        cr = [column(mr[near], 8 * t + j, lane) for j in range(8)]
        ci = [column(mi[near], 8 * t + j, lane) for j in range(8)]
        rr = jnp.where(inside, jnp.where(col == sub + 8 * t, 1.0, 0.0), mr[t])
        ri = jnp.where(inside, 0.0, mi[t])
        vr, vi = jnp.ones((8, 128), f32), jnp.zeros((8, 128), f32)
        for k in range(8):
            at = sub == k
            pr, pi = row(xr[k], k), row(xi[k], k)
            q = 1.0 / (pr * pr + pi * pi)
            er, ei = jnp.where(at, 0.0, xr[k]), jnp.where(at, 0.0, xi[k])
            fr, fi = er * pr + ei * pi, ei * pr - er * pi
            vr, vi = jnp.where(at, pr * q, vr), jnp.where(at, -(pi * q), vi)

            def step(yr, yi):
                ar, ai = row(yr, k), row(yi, k)
                wr, wi = fr * ar - fi * ai, fr * ai + fi * ar
                return yr - wr * q, yi - wi * q

            for j in range(k + 1, 8):
                xr[j], xi[j] = step(xr[j], xi[j])
            rr, ri = step(rr, ri)
        rr, ri = rr * vr - ri * vi, rr * vi + ri * vr
        lines = [(row(rr, j), row(ri, j)) for j in range(8)]
        more_r = added([cr[j] * lines[j][0] - ci[j] * lines[j][1] for j in range(8)])
        more_i = added([cr[j] * lines[j][1] + ci[j] * lines[j][0] for j in range(8)])
        mr[near] = jnp.where(inside, 0.0, mr[near]) - more_r
        mi[near] = jnp.where(inside, 0.0, mi[near]) - more_i
        out_r, out_i = far_product([mr[s] for s in far], [mi[s] for s in far], rr, ri, t)
        for n, s in enumerate(far):
            mr[s] = jnp.where(inside, 0.0, mr[s]) - out_r[8 * n : 8 * n + 8]
            mi[s] = jnp.where(inside, 0.0, mi[s]) - out_i[8 * n : 8 * n + 8]
        mr[t], mi[t] = rr, ri
        yield


def slabs(x):
    return [x[8 * s : 8 * s + 8] for s in range(8)]


def invert_pairs(pairs, beside=()):
    beside = iter(beside)
    held = [(slabs(zr), slabs(zi)) for zr, zi in pairs]
    for _ in zip(*[panels(mr, mi) for mr, mi in held]):
        work = next(beside, None)
        if work is not None:
            work()
    for work in beside:
        work()
    return [(jnp.concatenate(mr, 0), jnp.concatenate(mi, 0)) for mr, mi in held]


def low_lanes(x):
    return lax.broadcasted_iota(jnp.int32, x.shape, 1) < 64


def split(x):
    high = x.astype(bf16)
    return high, (x - high.astype(f32)).astype(bf16)


def diagonal(x):
    keep = low_lanes(x)
    zero = jnp.zeros_like(x)
    return jnp.concatenate([jnp.where(keep, x, zero), jnp.where(keep, zero, x)], 0)


def dot(a, b):
    return jnp.dot(a, b, preferred_element_type=f32)


def left_factor(qr, qi):
    rh, rl = split(qr)
    ih, il = split(qi)

    def whole(r, i):
        return jnp.concatenate(
            [jnp.concatenate([r, -i], 1), jnp.concatenate([i, r], 1)], 0
        )

    return jnp.concatenate([whole(rh, ih), whole(rl, il)], 0)


def right_factor(yr, yi):
    def whole(r, i):
        dr, di = diagonal(r), diagonal(i)
        return jnp.concatenate(
            [jnp.concatenate([dr, di], 1), jnp.concatenate([-di, dr], 1)], 0
        )

    rh, rl = split(yr)
    ih, il = split(yi)
    return whole(rh, ih), whole(rl, il)


def times_right(xr, xi, high, low):
    xh, xl = split(jnp.concatenate([xr, xi], 1))
    both = dot(jnp.concatenate([xh, xl], 0), high)
    out = both[:64] + (both[64:] + dot(xh, low))
    return out[:, :128], out[:, 128:]


def times_left(left, xr, xi):
    rh, rl = split(xr)
    ih, il = split(xi)
    right = jnp.concatenate(
        [
            jnp.concatenate([diagonal(rh), diagonal(rl)], 1),
            jnp.concatenate([diagonal(ih), diagonal(il)], 1),
        ],
        0,
    )
    out = dot(left, right)
    out = out[:128, :128] + (out[:128, 128:] + out[128:, :128])
    return out[:64], out[64:]


def swapped(x):
    return pltpu.roll(x, 64, 1)


def wire_kernel(segs, energy_ref, *refs):
    other = refs[:segs][::-1]
    own = refs[segs : 2 * segs][::-1]
    out_ref = refs[2 * segs]
    (u_ref, h_ref, d_ref, m_ref, at_ref, ar_ref, ai_ref, yright_ref, yleft_ref, g_ref, s_ref, k_ref, t_ref) = (
        refs[2 * segs + 1 :]
    )
    blocks = 2 * segs
    half = segs
    place, core = lax.axis_index("seg"), lax.axis_index("energy") & 1

    for k in range(segs):
        seg = jnp.bitwise_xor(place, k)
        for c, ref in ((core, own[k]), (1 - core, other[k])):
            u_ref[4 * seg + 2 * c] = ref[0:64]
            u_ref[4 * seg + 2 * c + 1] = ref[64:128]
            h_ref[2 * seg + c] = ref[128:192]
            d_ref[2 * seg + c] = ref[192:200]
        m_ref[seg] = own[k][200:208]
    energy = energy_ref[0]

    start = jnp.int32(0)
    first, used = jnp.int32(0), jnp.int32(0)
    for seg in range(segs):
        count = jnp.max(m_ref[seg, 4:5, :]).astype(jnp.int32)
        for k in range(4):
            at_ref[start + k] = 4 * seg + k
        first = jnp.where(seg == place, start, first)
        used = jnp.where(seg == place, count, used)
        start = start + count

    keep = low_lanes(jnp.zeros((64, 128), f32))
    rows = lax.broadcasted_iota(jnp.int32, (64, 128), 0)
    cols = lax.broadcasted_iota(jnp.int32, (64, 128), 1) & 63

    def prepare_block(i, carry):
        one, two = at_ref[i], at_ref[blocks - 1 - i]
        odd_one, odd_two = one & 1, two & 1
        raw_one, raw_two = h_ref[one >> 1], h_ref[two >> 1]
        flat_re = jnp.where(keep, raw_one, swapped(raw_two))
        flat_im = jnp.where(keep, swapped(raw_one), raw_two)
        turned = jnp.concatenate([raw_one, raw_two], 0).T
        odd = jnp.where(keep, odd_one, odd_two)
        held = ((rows >= cols).astype(jnp.int32) ^ odd) > 0
        line = jnp.where(keep[:8], d_ref[one >> 1], swapped(d_ref[two >> 1]))
        on = rows == cols
        real = jnp.where(held, flat_re, turned[:64])
        real = jnp.where(on & (odd > 0), jnp.concatenate([line] * 8, 0), real)
        imag = jnp.where(on, 0.0, jnp.where(held, flat_im, -turned[64:]))
        extra = []
        for base in (0, 2):
            line_one = m_ref[one >> 2, pl.ds(base + ((one >> 1) & 1), 1), :]
            line_two = m_ref[two >> 2, pl.ds(base + ((two >> 1) & 1), 1), :]
            line_one = pltpu.roll(jnp.broadcast_to(line_one, (8, 128)), 64 * odd_one, 1)
            line_two = pltpu.roll(jnp.broadcast_to(line_two, (8, 128)), 64 * (1 - odd_two), 1)
            line = jnp.where(keep[:8], line_one, line_two)
            extra.append(jnp.broadcast_to(line[:1], (64, 128)))
        ar_ref[i] = jnp.where(on, energy - extra[0], 0.0) - real
        ai_ref[i] = jnp.where(on, broadening + extra[1], 0.0) - imag
        return carry

    def prepare_link(i, carry):
        one, two = u_ref[at_ref[i]], u_ref[at_ref[blocks - i]]
        flat_re = jnp.where(keep, one, swapped(two))
        flat_im = jnp.where(keep, swapped(one), two)
        turned = jnp.concatenate([one, two], 0).T
        turned_re, turned_im = turned[:64], -turned[64:]
        y = jnp.where(keep, flat_re, turned_re), jnp.where(keep, flat_im, turned_im)
        y_adjoint = jnp.where(keep, turned_re, flat_re), jnp.where(keep, turned_im, flat_im)
        high, low = right_factor(*y)
        yright_ref[i - 1, 0] = high
        yright_ref[i - 1, 1] = low
        yleft_ref[i - 1] = left_factor(*y_adjoint)
        return y, y_adjoint

    def long_wire():
        lax.fori_loop(0, half, prepare_block, 0)
        lax.fori_loop(1, half + 1, lambda i, carry: prepare_link(i, carry) and carry, 0)

        s_ref[...] = jnp.zeros_like(s_ref)

        def inward(i, carry):
            fr = ar_ref[i] - s_ref[0]
            fi = ai_ref[i] - s_ref[1]
            ((gr, gi),) = invert_pairs([(fr, fi)])
            g_ref[i, 0] = gr
            g_ref[i, 1] = gi

            @pl.when(i < half)
            def _():
                tr, ti = times_right(gr, gi, yright_ref[i, 0], yright_ref[i, 1])
                t_ref[i] = left_factor(tr, ti)
                sr, si = times_left(yleft_ref[i], tr, ti)
                kr, ki = times_left(yleft_ref[i], gr, gi)
                high, low = right_factor(kr, ki)
                k_ref[i, 0] = high
                k_ref[i, 1] = low
                s_ref[0] = sr
                s_ref[1] = si

            @pl.when(i == half - 1)
            def _():
                s_ref[0] = swapped(s_ref[0])
                s_ref[1] = swapped(s_ref[1])
                ar_ref[half] = fr
                ai_ref[half] = fi

            return carry

        lax.fori_loop(0, half + 1, inward, 0)

        g_ref[half - 1] = g_ref[half]

        def outward(step, carry):
            i = half - 2 - step
            zr, zi = times_right(g_ref[i + 1, 0], g_ref[i + 1, 1], k_ref[i, 0], k_ref[i, 1])
            wr, wi = times_left(t_ref[i], zr, zi)
            g_ref[i, 0] = g_ref[i, 0] + wr
            g_ref[i, 1] = g_ref[i, 1] + wi
            return carry

        lax.fori_loop(0, half - 1, outward, 0)

    def wire_of_eight():
        v = {}

        def plus(x, y):
            return x[0] + y[0], x[1] + y[1]

        def minus(x, y):
            return x[0] - y[0], x[1] - y[1]

        def block(i):
            return ar_ref[i], ai_ref[i]

        def by_y(x, i):
            return times_right(*x, yright_ref[i - 1, 0], yright_ref[i - 1, 1])

        def adjoint_y_by(i, x):
            return times_left(yleft_ref[i - 1], *x)

        def do(step, *args):
            return lambda: step(*args)

        def link_two():
            y, y_adjoint = prepare_link(2, 0)
            v["y2_left"] = left_factor(*y)
            v["y2_adjoint_right"] = right_factor(*y_adjoint)

        def hold(name, product, *names):
            def run():
                v[name] = product(*[v[x] for x in names])

            return run

        def left_form(x):
            return left_factor(*x)

        def right_form(x):
            return right_factor(*x)

        def left_times(left, x):
            return times_left(left, *x)

        def times_right_form(x, right):
            return times_right(*x, *right)

        prepare_block(0, 0)
        prepare_block(2, 0)
        v["g0"], v["g2"] = invert_pairs(
            [block(0), block(2)],
            [
                do(prepare_link, 1, 0),
                link_two,
                do(prepare_block, 1, 0),
                do(prepare_link, 3, 0),
                do(prepare_block, 3, 0),
                do(prepare_link, 4, 0),
            ],
        )
        v["t0"] = by_y(v["g0"], 1)
        v["p_"] = left_times(v["y2_left"], v["g2"])
        first_one = minus(block(1), adjoint_y_by(1, v["t0"]))
        first_one = minus(first_one, times_right_form(v["p_"], v["y2_adjoint_right"]))

        def third():
            v["q_"] = adjoint_y_by(3, v["g2"])

        def fourth():
            v["f3"] = minus(block(3), by_y(v["q_"], 3))

        def w13():
            v["w13"] = right_form(by_y(v["p_"], 3))

        def w31():
            v["w31"] = left_form(times_right_form(v["q_"], v["y2_adjoint_right"]))

        def k0():
            v["k0"] = right_form(adjoint_y_by(1, v["g0"]))

        def q():
            v["q"] = by_y(v["g2"], 3)

        def p():
            v["p"] = left_form(times_right_form(v["g2"], v["y2_adjoint_right"]))

        def forms():
            v["t0_left"] = left_form(v["t0"])
            v["p_right"] = right_form(v["p_"])

        (v["g1"],) = invert_pairs([first_one], [third, w13, w31, fourth, k0, q, p, forms])
        v["m"] = times_right_form(v["g1"], v["w13"])
        f3 = minus(v["f3"], left_times(v["w31"], v["m"]))

        def base_zero():
            v["base0"] = plus(v["g0"], times_right_form(v["t0_g1"], v["k0"]))

        def base_two():
            v["base2"] = plus(v["g2"], times_right_form(v["p_g1"], v["p_right"]))

        def left_two():
            v["left2"] = left_form(plus(left_times(v["p"], v["m"]), v["q"]))

        def right_two():
            v["right2"] = right_form(plus(times_right_form(v["n"], v["p_right"]), v["q_"]))

        def left_zero():
            v["left0"] = left_form(left_times(v["t0_left"], v["m"]))

        def right_zero():
            v["right0"] = right_form(times_right_form(v["n"], v["k0"]))

        def ends():
            v["left1"] = left_form(v["m"])
            v["right1"] = right_form(v["n"])

        (g3,) = invert_pairs(
            [f3],
            [
                hold("n", left_times, "w31", "g1"),
                hold("t0_g1", left_times, "t0_left", "g1"),
                hold("p_g1", left_times, "p", "g1"),
                base_zero,
                base_two,
                left_two,
                right_two,
                ends,
            ],
        )
        across = adjoint_y_by(4, by_y(g3, 4))
        middle = minus(f3, (swapped(across[0]), swapped(across[1])))
        (g_middle,) = invert_pairs([middle], [left_zero, right_zero])
        g_ref[3, 0], g_ref[3, 1] = g_middle
        for i, base in ((0, "base0"), (1, "g1"), (2, "base2")):
            more = times_right_form(g_middle, v["right" + str(i)])
            g_ref[i, 0], g_ref[i, 1] = plus(v[base], left_times(v["left" + str(i)], more))

    if half == 4:
        wire_of_eight()
    else:
        long_wire()

    for k in range(4):
        block = jnp.minimum(first + k, blocks - 1)
        right = (block >= half).astype(jnp.int32)
        i = jnp.where(block >= half, blocks - 1 - block, block)
        re = pltpu.roll(g_ref[i, 0], 64 * right, 1)
        im = pltpu.roll(g_ref[i, 1], 64 * (1 - right), 1)
        live = (k < used).astype(f32)
        out_ref[k] = (jnp.where(keep, re, im) * live).astype(bf16)


def wire(energies, own, other):
    segs = len(own)
    half = segs

    def kernel(*refs):
        wire_kernel(segs, *refs)

    return pl.pallas_call(
        kernel,
        out_shape=jax.ShapeDtypeStruct((4, 64, 128), bf16),
        in_specs=[SMEM] + [VMEM] * (2 * segs),
        out_specs=VMEM,
        scratch_shapes=[
            pltpu.VMEM((4 * segs, 64, 128), f32),
            pltpu.VMEM((2 * segs, 64, 128), f32),
            pltpu.VMEM((2 * segs, 8, 128), f32),
            pltpu.VMEM((segs, 8, 128), f32),
            pltpu.SMEM((2 * segs + 4,), jnp.int32),
            pltpu.VMEM((half + 1, 64, 128), f32),
            pltpu.VMEM((half + 1, 64, 128), f32),
            pltpu.VMEM((half, 2, 256, 256), bf16),
            pltpu.VMEM((half, 256, 256), bf16),
            pltpu.VMEM((half + 1, 2, 64, 128), f32),
            pltpu.VMEM((2, 64, 128), f32),
            pltpu.VMEM((half, 2, 256, 256), bf16),
            pltpu.VMEM((half, 256, 256), bf16),
        ],
        compiler_params=pltpu.CompilerParams(vmem_limit_bytes=(8 + 2 * segs) * 2**20),
        name="wire",
    )(energies, *other[::-1], *own[::-1])


def order_kernel(chips, sources_ref, screened_ref, *out_refs):
    energy = lax.axis_index("energy")
    for side, (plain_ref, other_ref) in enumerate((out_refs[:2], out_refs[2:])):
        for k in range(chips):
            wanted = ((energy >> 1) ^ k) * cores + ((energy & 1) ^ side)
            place, found = jnp.int32(0), jnp.int32(0)
            for j in range(screened_ref.shape[0]):
                hit = (sources_ref[0, j] == wanted).astype(jnp.int32)
                place, found = place + j * hit, found + hit
            for slot in range(4):
                weight = screened_ref[place, slot] * found.astype(f32)
                plain_ref[k, slot] = weight
                other_ref[k, slot] = swapped(weight)


def order_weights(chips, sources, screened):
    shape = jax.ShapeDtypeStruct((chips,) + screened.shape[1:], f32)

    def kernel(*refs):
        order_kernel(chips, *refs)

    return pl.pallas_call(
        kernel,
        out_shape=[shape] * 4,
        in_specs=[SMEM, VMEM],
        out_specs=[VMEM] * 4,
        compiler_params=pltpu.CompilerParams(vmem_limit_bytes=(4 + chips) * 2**20),
        name="order_weights",
    )(sources, screened)


def sum_kernel(pieces, plain_ref, other_ref, *refs):
    greens, rest = refs[:pieces], refs[pieces:]
    keep = low_lanes(jnp.zeros((64, 128), f32))

    def total(slot):
        direct = jnp.zeros((64, 128), f32)
        crossed = jnp.zeros((64, 128), f32)
        for k in range(pieces):
            green = greens[k][slot].astype(f32)
            direct = direct + green * plain_ref[k, slot]
            crossed = crossed + green * other_ref[k, slot]
        return jnp.where(keep, direct - swapped(direct), crossed + swapped(crossed))

    if len(rest) == 1:
        for slot in range(4):
            rest[0][slot] = total(slot)
    else:
        before_ref, out_ref, done_ref, sem = rest
        copies = []
        for slot in range(4):
            done_ref[slot] = total(slot) + before_ref[slot]
            copies.append(pltpu.make_async_copy(done_ref.at[slot], out_ref.at[slot], sem.at[slot]))
            copies[-1].start()
        for copy in copies:
            copy.wait()


def sum_near(greens, plain, other):
    def kernel(*refs):
        sum_kernel(len(greens), *refs)

    return pl.pallas_call(
        kernel,
        out_shape=jax.ShapeDtypeStruct(plain.shape[1:], f32),
        in_specs=[VMEM] * (2 + len(greens)),
        out_specs=VMEM,
        compiler_params=pltpu.CompilerParams(vmem_limit_bytes=(4 + len(greens)) * 2**20),
        name="sum_near",
    )(plain, other, *greens)


def sum_far(greens, plain, other, before):
    def kernel(*refs):
        sum_kernel(len(greens), *refs)

    return pl.pallas_call(
        kernel,
        out_shape=jax.ShapeDtypeStruct(plain.shape[1:], f32),
        in_specs=[VMEM] * (3 + len(greens)),
        out_specs=pl.BlockSpec(memory_space=pl.ANY),
        scratch_shapes=[pltpu.VMEM(plain.shape[1:], f32), pltpu.SemaphoreType.DMA((4,))],
        compiler_params=pltpu.CompilerParams(vmem_limit_bytes=(4 + len(greens)) * 2**20),
        name="sum_far",
    )(plain, other, *greens, before)


def flipped_to(x, axis, mask):
    count = lax.axis_size(axis)
    return lax.ppermute(x, axis, [(i, i ^ mask) for i in range(count)])


def body(energies, h_blocks, couplings, shift_real, shift_rate, screened, sources, counts):
    segs = lax.axis_size("seg")
    chips = lax.axis_size("energy") // cores
    first = lax.axis_index("energy") % cores == 0
    hams, links = h_blocks[0], couplings[0]
    one = jnp.where(first, hams[0], hams[2])
    two = jnp.where(first, hams[1], hams[3])
    lower = jnp.arange(64)[:, None] >= jnp.arange(128)[None, :] % 64
    group = jnp.arange(128)[None, :] % 64 // 8
    line = sum(jnp.where(group == n, two[8 * n : 8 * n + 8], 0.0) for n in range(8))

    def at_rows(x, start):
        return jnp.pad(x, ((start, 208 - start - x.shape[0]), (0, 0)))

    piece = (
        at_rows(jnp.where(first, links[0], links[2]), 0)
        + at_rows(jnp.where(first, links[1], links[3]), 64)
        + at_rows(jnp.where(lower, one, two), 128)
        + at_rows(line, 192)
        + at_rows(shift_real.reshape(2, 128), 200)
        + at_rows(shift_rate.reshape(2, 128), 202)
        + at_rows(jnp.broadcast_to(counts.astype(f32)[:, None], (4, 128)), 204)
    )
    sent = [flipped_to(piece, "seg", k) for k in range(1, segs)]
    own = [piece] + sent
    other = [flipped_to(x, "energy", 1) for x in [piece] + sent]
    greens = wire(energies, own, other)
    near = [greens] + [flipped_to(greens, "energy", cores * k) for k in range(1, chips)]
    far = [flipped_to(x, "energy", 1) for x in near]
    plain_near, other_near, plain_far, other_far = order_weights(chips, sources, screened[:, 0])
    partial = sum_near(near, plain_near, other_near)
    return sum_far(far, plain_far, other_far, partial)[None, None]


def solution(mesh):
    in_specs = (
        P("energy"),
        P("seg", None, None, None),
        P("seg", None, None, None),
        P("energy", "seg", None),
        P("energy", "seg", None),
        P(None, "seg", None, None, None),
        P("energy", None),
        P("seg"),
    )
    out_specs = P("energy", "seg", None, None, None)
    return jax.shard_map(body, mesh=mesh, in_specs=in_specs, out_specs=out_specs, check_vma=False)
```
